32 devices in a mesh: dp: 8 (over y, x, core), mp: 4 (over z).
Axes of the slice: x: 2, y: 2, z: 4, core: 2. Of those that a mesh axis runs over, the one named last changes fastest.
Arguments:
- tokens: bfloat16 [8192, 2048], P(('dp', 'mp')), may hold values from -6 to 6
- norm_gain: float32 [2048], replicated, may hold values from 0.1 to 1.9
- mlp_gain: float32 [2048], replicated, may hold values from 0.1 to 1.9
- lengths: int32 [8], P('dp'), may hold values from 1 to 1024, as said below
- log_decay: float32 [8192, 8], P('dp'), as said below
- query_master: float32 [2048, 2048], P(('dp', 'mp')), may hold values from -0.125 to 0.125
- key_master: float32 [2048, 2048], P(('dp', 'mp')), may hold values from -0.125 to 0.125
- value_master: float32 [2048, 4096], P(('dp', 'mp')), may hold values from -0.125 to 0.125
- swish_master: float32 [2048, 4096], P(('dp', 'mp')), may hold values from -0.125 to 0.125
- output_master: float32 [4096, 2048], P(None, ('dp', 'mp')), may hold values from -0.09375 to 0.09375
- ffn_gate_master: float32 [2048, 4096], P(('dp', 'mp')), may hold values from -0.125 to 0.125
- ffn_up_master: float32 [2048, 4096], P(('dp', 'mp')), may hold values from -0.125 to 0.125
Outputs:
- residual: bfloat16 [8192, 2048], P(('dp', 'mp'))
- hidden: bfloat16 [8192, 4096], P('dp', 'mp')
The draws below stay inside these ranges and needn't reach their ends.
Inputs may be any that keep to these rules, and one draw needn't show every extreme that they name: `lengths`: given length of each prompt; in every draw some prompt has exactly 1024 tokens and some has 1. `log_decay`: Negative.
All inputs are finite; a program needn't handle non-finite values.
Results may differ from the reference program's by a relative error of at most 0.023.
Values may be sent and summed in bfloat16 or wider, within the bound.
No kernel may reach another device: no remote copies, remote signals or barrier semaphores. Data moves between devices by JAX's collectives and lax.ppermute only.
A program may use at most 128 MiB of HBM per device.

```python
import math
import jax
import jax.numpy as jnp
from jax import lax

D = 2048
H = 8
DK = 256
DV = 512
FF = 4096
REQUEST_SPAN = 1024
KEYS = 2048
VALS = 4096
REQUEST_TOTAL = 8
TOKENS = 8192


def draw_lengths(key, part):
    first_key, second_key = jax.random.split(key)
    drawn_numbers = jax.random.randint(first_key, (REQUEST_TOTAL,), 1, REQUEST_SPAN + 1)
    chosen = jax.random.permutation(second_key, REQUEST_TOTAL)
    drawn_numbers = drawn_numbers.at[chosen[0]].set(REQUEST_SPAN)
    drawn_numbers = drawn_numbers.at[chosen[1]].set(1)
    return drawn_numbers.astype(jnp.int32)


def draw_log_decay(key, part):
    fading_seed_handle, coarse_seed_handle, spike_seed_handle, fill_seed_handle = jax.random.split(key, 4)
    lowest, highest = (math.log(0.2 / REQUEST_SPAN), math.log(30.0 / REQUEST_SPAN))
    depth_low = 0.5
    fading_factors = jnp.exp(jax.random.uniform(fading_seed_handle, (REQUEST_TOTAL, 1, H), jnp.float32, lowest, highest))
    coarse_spans = jax.random.uniform(coarse_seed_handle, (REQUEST_TOTAL, REQUEST_SPAN, H), jnp.float32, 0.5, 1.5)
    spike_spans = jax.random.randint(spike_seed_handle, (REQUEST_TOTAL, REQUEST_SPAN, 1), 0, REQUEST_SPAN) < 3
    request_fill_level = jnp.log(jax.random.uniform(fill_seed_handle, (REQUEST_TOTAL, REQUEST_SPAN, H), jnp.float32, depth_low, 0.8))
    drawn_numbers = -fading_factors * coarse_spans + jnp.where(spike_spans, request_fill_level, 0.0)
    return drawn_numbers.reshape(REQUEST_TOTAL * REQUEST_SPAN, H).astype(jnp.float32)


def shard_levels(key, shape, cuts, low, top_value):
    loudness, own = 1.0, jax.random.fold_in(key, 6)
    for dim, parts in cuts:
        draws = jnp.exp(jax.random.uniform(jax.random.fold_in(own, dim), (parts,), jnp.float32, low / len(cuts), top_value / len(cuts)))
        loudness = loudness * jnp.repeat(draws, shape[dim] // parts).reshape([-1 if axis == dim else 1 for axis in range(len(shape))])
    return loudness


def scatter_about(rng, shape, deviation, limit, cuts=(), held_as=jnp.bfloat16):
    loudness = shard_levels(rng, shape, cuts, -0.22, 0.18) if cuts else 1.0
    values = jax.random.normal(rng, shape, jnp.float32) * deviation * loudness
    return jnp.minimum(jnp.maximum(values, -limit), limit).astype(held_as)


def setup_inputs(seed: int = 0) -> dict:
    splits = jax.random.split(jax.random.key(seed), 13)
    return {
        "tokens": scatter_about(splits[0], (TOKENS, D), 1.0, 6.0, ((0, 32),)),
        "norm_gain": jnp.clip(1.0 + 0.18 * jax.random.normal(splits[1], (D,), jnp.float32), 0.1, 1.9),
        "mlp_gain": jnp.clip(1.0 + 0.18 * jax.random.normal(splits[2], (D,), jnp.float32), 0.1, 1.9),
        "lengths": draw_lengths(jax.random.fold_in(splits[12], 71), 0),
        "log_decay": draw_log_decay(jax.random.fold_in(splits[12], 71), 0),
        "query_master": scatter_about(splits[5], (D, KEYS), D ** -0.5, 0.125, ((0, 32),), jnp.float32),
        "key_master": scatter_about(splits[6], (D, KEYS), D ** -0.5, 0.125, ((0, 32),), jnp.float32),
        "value_master": scatter_about(splits[7], (D, VALS), D ** -0.5, 0.125, ((0, 32),), jnp.float32),
        "swish_master": scatter_about(splits[8], (D, VALS), D ** -0.5, 0.125, ((0, 32),), jnp.float32),
        "output_master": scatter_about(splits[9], (VALS, D), VALS ** -0.5, 0.09375, ((1, 32),), jnp.float32),
        "ffn_gate_master": scatter_about(splits[10], (D, FF), D ** -0.5, 0.125, ((0, 32),), jnp.float32),
        "ffn_up_master": scatter_about(splits[11], (D, FF), D ** -0.5, 0.125, ((0, 32),), jnp.float32),
    }


def rms_rows(row_block, gain_vec):
    values = row_block.astype(jnp.float32)
    scale = lax.rsqrt(lax.optimization_barrier(jnp.mean(values * values, axis=-1, keepdims=True)) + 1e-06)
    return (values * scale * gain_vec.astype(jnp.float32)).astype(jnp.bfloat16)

def rotate(values, places, first_channel):
    columns = values.shape[1]
    channel = (first_channel + jnp.arange(columns, dtype=jnp.int32)) % DK
    paired = (channel // 2 * 2).astype(jnp.float32)
    frequency = jnp.exp(paired * (-math.log(10000.0) / DK))
    angles = places.astype(jnp.float32)[:, None] * frequency[None, :]
    couples = values.reshape(values.shape[0], columns // 2, 2)
    turned = jnp.stack([-couples[:, :, 1], couples[:, :, 0]], axis=-1).reshape(values.shape)
    return values * jnp.cos(angles) + turned * jnp.sin(angles)

def retain_prompt(prompt_items):
    q_prompt, k_prompt, v_prompt, running = prompt_items
    scores = jnp.einsum('thd,shd->hts', q_prompt.astype(jnp.float32), k_prompt.astype(jnp.float32)) * DK ** (-0.5)
    decay_gap = running.T[:, :, None] - running.T[:, None, :]
    causal_mask = jnp.arange(REQUEST_SPAN, dtype=jnp.int32)[:, None] >= jnp.arange(REQUEST_SPAN, dtype=jnp.int32)[None, :]
    weights = (scores * jnp.exp(jnp.where(causal_mask[None], decay_gap, -jnp.inf))).astype(jnp.bfloat16)
    return jnp.einsum('hts,shd->thd', weights.astype(jnp.float32), v_prompt.astype(jnp.float32))

def reference(tokens, norm_gain, mlp_gain, lengths, log_decay, query_master, key_master, value_master, swish_master, output_master, ffn_gate_master, ffn_up_master):
    normed_in = rms_rows(tokens, norm_gain)
    places = jnp.arange(TOKENS, dtype=jnp.int32) % REQUEST_SPAN
    queries = rotate(jnp.dot(normed_in, query_master.astype(jnp.bfloat16), preferred_element_type=jnp.float32), places, 0).astype(jnp.bfloat16)
    key_rows = rotate(jnp.dot(normed_in, key_master.astype(jnp.bfloat16), preferred_element_type=jnp.float32), places, 0).astype(jnp.bfloat16)
    value_rows = jnp.dot(normed_in, value_master.astype(jnp.bfloat16), preferred_element_type=jnp.float32).astype(jnp.bfloat16)
    gate_rows = jnp.dot(normed_in, swish_master.astype(jnp.bfloat16), preferred_element_type=jnp.float32).astype(jnp.bfloat16)
    running = jnp.cumsum(log_decay.reshape(REQUEST_TOTAL, REQUEST_SPAN, H), axis=1)
    retained = lax.map(retain_prompt, (queries.reshape(REQUEST_TOTAL, REQUEST_SPAN, H, DK), key_rows.reshape(REQUEST_TOTAL, REQUEST_SPAN, H, DK), value_rows.reshape(REQUEST_TOTAL, REQUEST_SPAN, H, DV), running))
    channel_mean = lax.optimization_barrier(jnp.mean(retained, axis=-1, keepdims=True))
    spread = lax.optimization_barrier(jnp.mean(retained * retained, axis=-1, keepdims=True)) - channel_mean * channel_mean
    normed_heads = ((retained - channel_mean) * lax.rsqrt(spread + 1e-05)).reshape(TOKENS, VALS)
    live_rows = places < jnp.repeat(lengths, REQUEST_SPAN)
    gated = jnp.where(live_rows[:, None], jax.nn.silu(gate_rows.astype(jnp.float32)) * normed_heads, 0.0).astype(jnp.bfloat16)
    branch = jnp.dot(gated, output_master.astype(jnp.bfloat16), preferred_element_type=jnp.float32)
    residual = (tokens.astype(jnp.float32) + branch).astype(jnp.bfloat16)
    normed_mid = rms_rows(residual, mlp_gain)
    gate_part = jnp.dot(normed_mid, ffn_gate_master.astype(jnp.bfloat16), preferred_element_type=jnp.float32)
    up_part = jnp.dot(normed_mid, ffn_up_master.astype(jnp.bfloat16), preferred_element_type=jnp.float32)
    hidden = (jax.nn.silu(gate_part) * up_part).astype(jnp.bfloat16)
    return (residual, hidden)
```

```python
import math

import jax
import jax.numpy as jnp
from jax import lax
from jax.experimental import pallas as pl
from jax.experimental.pallas import tpu as pltpu
from jax.sharding import PartitionSpec as P

H = 8
DK = 256
DV = 512
SPAN = 1024
HALF = DK // 2
ROWS = 256
BF = jnp.bfloat16
F32 = jnp.float32


def rms_rows(row_block, gain_vec):
    values = row_block.astype(F32)
    scale = lax.rsqrt(jnp.mean(values * values, axis=-1, keepdims=True) + 1e-06)
    return (values * scale * gain_vec).astype(BF)


def even_odd(matrix):
    rows = matrix.shape[0]
    new = jnp.arange(DK, dtype=jnp.int32)
    old = jnp.where(new < HALF, 2 * new, 2 * (new - HALF) + 1)
    one_hot = (jnp.arange(DK, dtype=jnp.int32)[:, None] == old[None, :]).astype(BF)
    heads = matrix.reshape(rows * H, DK)
    return jnp.dot(heads, one_hot, preferred_element_type=F32).astype(BF).reshape(rows, H * DK)


def by_owner(matrix, width, share, mp_count):
    rows = matrix.shape[0]
    if share > 1:
        heads = jnp.repeat(matrix.reshape(rows, H, width), share, axis=1)
        return heads.transpose(1, 0, 2)
    return matrix.reshape(rows, mp_count, -1).transpose(1, 0, 2)


def ring_gather(block, count):
    order = [(i, (i + 1) % count) for i in range(count)]
    blocks = [block]
    for _ in range(count - 1):
        blocks.append(lax.ppermute(blocks[-1], "mp", order))
    return blocks


def in_order(blocks, index):
    count, rows = len(blocks), blocks[0].shape[0]
    whole = jnp.zeros((count * rows, blocks[0].shape[1]), blocks[0].dtype)
    for step, block in enumerate(blocks):
        whole = lax.dynamic_update_slice_in_dim(whole, block, (index - step) % count * rows, 0)
    return whole


def ring_sum(parts, index, count):
    rows = parts.shape[0] // count
    order = [(i, (i + 1) % count) for i in range(count)]

    def part(place):
        return lax.dynamic_slice_in_dim(parts, place % count * rows, rows, 0).astype(F32)

    total = part(index - 1)
    for step in range(count - 1):
        moved = lax.ppermute(total.astype(BF), "mp", order)
        total = moved.astype(F32) + part(index - 2 - step)
    return total


def retention_kernel(dims, scalars, x_ref, cos_ref, sin_ref, run_col, run_row, w_ref, wo_ref, out_ref, k_all, v_all):
    heads, share, wq, wv, wg = dims
    step = pl.program_id(0)
    x = x_ref[...]
    cos, sin = cos_ref[...], sin_ref[...]

    def turned(first):
        a, b = first[:, :HALF], first[:, HALF:]
        return a * cos - b * sin, b * cos + a * sin

    rows = pl.ds(pl.multiple_of(step * ROWS, ROWS), ROWS)
    queries = []
    for h in range(heads):
        q0, q1 = turned(jnp.dot(x, w_ref[:, h * DK : (h + 1) * DK], preferred_element_type=F32))
        queries.append((q0 * DK**-0.5, q1 * DK**-0.5))
        k0, k1 = turned(jnp.dot(x, w_ref[:, wq + h * DK : wq + (h + 1) * DK], preferred_element_type=F32))
        k_all[rows, h * DK : h * DK + HALF] = k0.astype(BF)
        k_all[rows, h * DK + HALF : (h + 1) * DK] = k1.astype(BF)
    v_all[rows, :] = jnp.dot(x, w_ref[:, 2 * wq : 2 * wq + wv], preferred_element_type=F32).astype(BF)
    gate = jnp.dot(x, w_ref[:, 2 * wq + wv :], preferred_element_type=F32).astype(BF).astype(F32)
    gate = gate / (1.0 + jnp.exp(-gate))
    place = step * ROWS + lax.broadcasted_iota(jnp.int32, (ROWS, 1), 0)
    gate = jnp.where(place < scalars[0], gate, 0.0)
    live = place < scalars[0]

    for now in range(SPAN // ROWS):

        @pl.when(step == now)
        def _():
            seen = (now + 1) * ROWS
            pieces = []
            for h in range(heads):
                q = jnp.concatenate([queries[h][0].astype(BF), queries[h][1].astype(BF)], axis=1)
                scores = lax.dot_general(
                    q, k_all[:seen, h * DK : (h + 1) * DK], (((1,), (1,)), ((), ())), preferred_element_type=F32
                )
                gap = run_col[:, h : h + 1] - run_row[h : h + 1, :seen]
                t = now * ROWS + lax.broadcasted_iota(jnp.int32, (ROWS, seen), 0)
                s = lax.broadcasted_iota(jnp.int32, (ROWS, seen), 1)
                weights = (scores * jnp.exp(jnp.where(t >= s, gap, -jnp.inf))).astype(BF)
                kept = jnp.dot(weights, v_all[:seen, h * DV : (h + 1) * DV], preferred_element_type=F32)
                mean = jnp.mean(kept, axis=-1, keepdims=True)
                spread = jnp.mean(kept * kept, axis=-1, keepdims=True) - mean * mean
                normed = (kept - mean) * lax.rsqrt(spread + 1e-05)
                if share > 1:
                    mine = normed[:, :wg]
                    for bit in range(1, share):
                        mine = jnp.where(scalars[1] == bit, normed[:, bit * wg : (bit + 1) * wg], mine)
                    normed = mine
                pieces.append(normed)
            whole = jnp.concatenate(pieces, axis=1) if heads > 1 else pieces[0]
            gated = jnp.where(live, gate * whole, 0.0).astype(BF)
            out_ref[...] = lax.dot_general(
                gated, wo_ref[...], (((1,), (1,)), ((), ())), preferred_element_type=F32
            ).astype(BF)


def retention(x, cos, sin, running, length, partner, w_in, w_out, heads, share):
    width = x.shape[1]
    wq, wv, wg = heads * DK, heads * DV, w_out.shape[1]
    dims = (heads, share, wq, wv, wg)
    scalars = jnp.stack([length, partner]).astype(jnp.int32)
    grid_spec = pltpu.PrefetchScalarGridSpec(
        num_scalar_prefetch=1,
        grid=(SPAN // ROWS,),
        in_specs=[
            pl.BlockSpec((ROWS, width), lambda i, _: (i, 0)),
            pl.BlockSpec((ROWS, HALF), lambda i, _: (i, 0)),
            pl.BlockSpec((ROWS, HALF), lambda i, _: (i, 0)),
            pl.BlockSpec((ROWS, heads), lambda i, _: (i, 0)),
            pl.BlockSpec((heads, SPAN), lambda i, _: (0, 0)),
            pl.BlockSpec(w_in.shape, lambda i, _: (0, 0), pipeline_mode=pl.Buffered(1)),
            pl.BlockSpec(w_out.shape, lambda i, _: (0, 0), pipeline_mode=pl.Buffered(1)),
        ],
        out_specs=pl.BlockSpec((ROWS, width), lambda i, _: (i, 0)),
        scratch_shapes=[pltpu.VMEM((SPAN, wq), BF), pltpu.VMEM((SPAN, wv), BF)],
    )
    return pl.pallas_call(
        lambda *refs: retention_kernel(dims, *refs),
        grid_spec=grid_spec,
        out_shape=jax.ShapeDtypeStruct((SPAN, width), BF),
        compiler_params=pltpu.CompilerParams(vmem_limit_bytes=48 * 2**20),
        cost_estimate=pl.CostEstimate(flops=20 * 10**9, bytes_accessed=26 * 10**6, transcendentals=2 * 10**6),
        name="retention",
    )(scalars, x, cos, sin, running, running.T, w_in, w_out)


def ffn_kernel(x_ref, w_ref, out_ref):
    width = out_ref.shape[1]
    x = x_ref[...]
    gate = jnp.dot(x, w_ref[:, :width], preferred_element_type=F32)
    up = jnp.dot(x, w_ref[:, width:], preferred_element_type=F32)
    out_ref[...] = (gate / (1.0 + jnp.exp(-gate)) * up).astype(BF)


def ffn(x, w):
    rows, width = x.shape
    out_width = w.shape[1] // 2
    return pl.pallas_call(
        ffn_kernel,
        grid=(rows // ROWS,),
        in_specs=[
            pl.BlockSpec((ROWS, width), lambda i: (i, 0)),
            pl.BlockSpec(w.shape, lambda i: (0, 0), pipeline_mode=pl.Buffered(1)),
        ],
        out_specs=pl.BlockSpec((ROWS, out_width), lambda i: (i, 0)),
        out_shape=jax.ShapeDtypeStruct((rows, out_width), BF),
        compiler_params=pltpu.CompilerParams(vmem_limit_bytes=40 * 2**20),
        cost_estimate=pl.CostEstimate(flops=2 * rows * width * w.shape[1], bytes_accessed=14 * 10**6, transcendentals=rows * out_width),
        name="ffn",
    )(x, w)


def per_device(
    tokens, norm_gain, mlp_gain, lengths, log_decay,
    query_master, key_master, value_master, swish_master, output_master, ffn_gate_master, ffn_up_master,
):
    mp_count = lax.axis_size("mp")
    mp_index = lax.axis_index("mp")
    share = max(1, mp_count // H)
    heads = max(1, H // mp_count)

    def handed_over(parts):
        block = jnp.concatenate(parts, axis=2)
        block = lax.all_to_all(block, "mp", split_axis=0, concat_axis=0, tiled=True)
        block = block.reshape(-1, block.shape[2])
        return lax.all_gather(block, "dp", axis=0, tiled=True)

    w_in = handed_over(
        [
            by_owner(even_odd(query_master.astype(BF)), DK, share, mp_count),
            by_owner(even_odd(key_master.astype(BF)), DK, share, mp_count),
            by_owner(value_master.astype(BF), DV, share, mp_count),
            by_owner(swish_master.astype(BF), DV, 1, mp_count),
        ]
    )
    w_out = handed_over([by_owner(output_master.astype(BF).T, DV, 1, mp_count)])
    w_ffn = handed_over(
        [by_owner(ffn_gate_master.astype(BF), DV, 1, mp_count), by_owner(ffn_up_master.astype(BF), DV, 1, mp_count)]
    )

    angles = jnp.arange(SPAN, dtype=jnp.int32).astype(F32)[:, None] * jnp.exp(
        (2 * jnp.arange(HALF, dtype=jnp.int32)).astype(F32) * (-math.log(10000.0) / DK)
    )
    cos, sin = jnp.cos(angles), jnp.sin(angles)
    first_head = mp_index // share * heads
    running = jnp.cumsum(lax.dynamic_slice_in_dim(log_decay, first_head, heads, 1), axis=0)

    normed_in = in_order(ring_gather(rms_rows(tokens, norm_gain), mp_count), mp_index)
    branch = retention(normed_in, cos, sin, running, lengths[0], mp_index % share, w_in, w_out, heads, share)
    residual = (tokens.astype(F32) + ring_sum(branch, mp_index, mp_count)).astype(BF)
    normed_mid = in_order(ring_gather(rms_rows(residual, mlp_gain), mp_count), mp_index)
    return residual, ffn(normed_mid, w_ffn)


def solution(mesh):
    rows, columns = P(("dp", "mp"), None), P(None, ("dp", "mp"))
    placed = (rows, P(), P(), P("dp"), P("dp", None), rows, rows, rows, rows, columns, rows, rows)
    return jax.shard_map(
        per_device, mesh=mesh, in_specs=placed, out_specs=(rows, P("dp", "mp")), check_vma=False
    )
```

```python
import math

import jax
import jax.numpy as jnp
from jax import lax
from jax.experimental import pallas as pl
from jax.experimental.pallas import tpu as pltpu
from jax.sharding import PartitionSpec as P

H = 8
DK = 256
DV = 512
SPAN = 1024
HALF = DK // 2
ROWS = 256
BF = jnp.bfloat16
F32 = jnp.float32


def rms_rows(row_block, gain_vec):
    values = row_block.astype(F32)
    scale = lax.rsqrt(jnp.mean(values * values, axis=-1, keepdims=True) + 1e-06)
    return (values * scale * gain_vec).astype(BF)


def even_odd(matrix):
    rows = matrix.shape[0]
    new = jnp.arange(DK, dtype=jnp.int32)
    old = jnp.where(new < HALF, 2 * new, 2 * (new - HALF) + 1)
    one_hot = (jnp.arange(DK, dtype=jnp.int32)[:, None] == old[None, :]).astype(BF)
    heads = matrix.reshape(rows * H, DK)
    return jnp.dot(heads, one_hot, preferred_element_type=F32).astype(BF).reshape(rows, H * DK)


def by_owner(matrix, width, share, mp_count):
    rows = matrix.shape[0]
    if share > 1:
        heads = jnp.repeat(matrix.reshape(rows, H, width), share, axis=1)
        return heads.transpose(1, 0, 2)
    return matrix.reshape(rows, mp_count, -1).transpose(1, 0, 2)


def ring_gather(block, count):
    order = [(i, (i + 1) % count) for i in range(count)]
    blocks = [block]
    for _ in range(count - 1):
        blocks.append(lax.ppermute(blocks[-1], "mp", order))
    return blocks


def in_order(blocks, index):
    count, rows = len(blocks), blocks[0].shape[0]
    whole = jnp.zeros((count * rows, blocks[0].shape[1]), blocks[0].dtype)
    for step, block in enumerate(blocks):
        whole = lax.dynamic_update_slice_in_dim(whole, block, (index - step) % count * rows, 0)
    return whole


def exchanged(block, index, count):
    pieces = []
    for shift in range(count):
        piece = lax.dynamic_index_in_dim(block, (index + shift) % count, 0, keepdims=False)
        if shift:
            piece = lax.ppermute(piece, "mp", [(i, (i + shift) % count) for i in range(count)])
        pieces.append(piece)
    return pieces


def ring_sum(parts, index, count):
    rows = parts.shape[0] // count
    order = [(i, (i + 1) % count) for i in range(count)]

    def part(place):
        return lax.dynamic_slice_in_dim(parts, place % count * rows, rows, 0).astype(F32)

    total = part(index - 1)
    for step in range(count - 1):
        moved = lax.ppermute(total.astype(BF), "mp", order)
        total = moved.astype(F32) + part(index - 2 - step)
    return total


def project_kernel(heads, scalars, x_ref, gain_ref, cos_ref, sin_ref, w_ref, *refs):
    normed_ref, out_ref = refs[-2:]
    wq = heads * DK
    x = rms_rows(x_ref[...], gain_ref[...])
    normed_ref[...] = x
    cos, sin = cos_ref[...], sin_ref[...]
    for h in range(2 * heads):
        low = h * DK
        both = jnp.dot(x, w_ref[:, low : low + DK], preferred_element_type=F32)
        a, b = both[:, :HALF], both[:, HALF:]
        scale = DK**-0.5 if h < heads else 1.0
        out_ref[:, low : low + HALF] = ((a * cos - b * sin) * scale).astype(BF)
        out_ref[:, low + HALF : low + DK] = ((b * cos + a * sin) * scale).astype(BF)
    out_ref[:, 2 * wq :] = jnp.dot(x, w_ref[:, 2 * wq :], preferred_element_type=F32).astype(BF)


def project(x, place, gain, cos, sin, w, heads, held):
    rows, width = x.shape
    out_width = w.shape[1]
    extra = [] if held is None else list(held)
    grid_spec = pltpu.PrefetchScalarGridSpec(
        num_scalar_prefetch=1,
        grid=(1,),
        in_specs=[
            pl.BlockSpec((rows, width), lambda i, s: (0, 0)),
            pl.BlockSpec((1, width), lambda i, s: (0, 0)),
            pl.BlockSpec((rows, HALF), lambda i, s: (s[0], 0)),
            pl.BlockSpec((rows, HALF), lambda i, s: (s[0], 0)),
            pl.BlockSpec(w.shape, lambda i, s: (0, 0)),
        ]
        + [pl.BlockSpec(memory_space=pl.ANY)] * len(extra),
        out_specs=[
            pl.BlockSpec((rows, width), lambda i, s: (s[0], 0)),
            pl.BlockSpec((rows, out_width), lambda i, s: (s[0], 0)),
        ],
    )
    return pl.pallas_call(
        lambda *refs: project_kernel(heads, *refs),
        grid_spec=grid_spec,
        out_shape=[jax.ShapeDtypeStruct((SPAN, width), BF), jax.ShapeDtypeStruct((SPAN, out_width), BF)],
        input_output_aliases={6: 0, 7: 1} if extra else {},
        compiler_params=pltpu.CompilerParams(vmem_limit_bytes=48 * 2**20),
        cost_estimate=pl.CostEstimate(
            flops=2 * rows * width * out_width, bytes_accessed=2 * (w.size + rows * (width + out_width)), transcendentals=0
        ),
        name="project",
    )(place.reshape(1).astype(jnp.int32), x, gain.reshape(1, -1), cos, sin, w, *extra)


def retention_kernel(dims, scalars, x_ref, run_col, run_row, qkv_ref, w_ref, out_ref):
    heads, share, wq, wv, wg = dims
    step = pl.program_id(0)
    gate = jnp.dot(x_ref[...], w_ref[:, :wg], preferred_element_type=F32).astype(BF).astype(F32)
    gate = gate / (1.0 + jnp.exp(-gate))
    live = step * ROWS + lax.broadcasted_iota(jnp.int32, (ROWS, 1), 0) < scalars[0]

    for now in range(SPAN // ROWS):

        @pl.when(step == now)
        def _():
            seen = (now + 1) * ROWS
            pieces = []
            for h in range(heads):
                scores = lax.dot_general(
                    qkv_ref[now * ROWS : seen, h * DK : (h + 1) * DK],
                    qkv_ref[:seen, wq + h * DK : wq + (h + 1) * DK],
                    (((1,), (1,)), ((), ())),
                    preferred_element_type=F32,
                )
                gap = run_col[:, h : h + 1] - run_row[h : h + 1, :seen]
                t = now * ROWS + lax.broadcasted_iota(jnp.int32, (ROWS, seen), 0)
                s = lax.broadcasted_iota(jnp.int32, (ROWS, seen), 1)
                weights = (scores * jnp.exp(jnp.where(t >= s, gap, -jnp.inf))).astype(BF)
                values = qkv_ref[:seen, 2 * wq + h * DV : 2 * wq + (h + 1) * DV]
                kept = jnp.dot(weights, values, preferred_element_type=F32)
                mean = jnp.mean(kept, axis=-1, keepdims=True)
                spread = jnp.mean(kept * kept, axis=-1, keepdims=True) - mean * mean
                normed = (kept - mean) * lax.rsqrt(spread + 1e-05)
                if share > 1:
                    mine = normed[:, :wg]
                    for bit in range(1, share):
                        mine = jnp.where(scalars[1] == bit, normed[:, bit * wg : (bit + 1) * wg], mine)
                    normed = mine
                pieces.append(normed)
            whole = jnp.concatenate(pieces, axis=1) if heads > 1 else pieces[0]
            gated = jnp.where(live, gate * whole, 0.0).astype(BF)
            out_ref[...] = lax.dot_general(
                gated, w_ref[:, wg:], (((1,), (1,)), ((), ())), preferred_element_type=F32
            ).astype(BF)


def retention(x, running, length, partner, qkv, w, heads, share):
    width = x.shape[1]
    wq, wv, wg = heads * DK, heads * DV, w.shape[1] // 2
    dims = (heads, share, wq, wv, wg)
    scalars = jnp.stack([length, partner]).astype(jnp.int32)
    grid_spec = pltpu.PrefetchScalarGridSpec(
        num_scalar_prefetch=1,
        grid=(SPAN // ROWS,),
        in_specs=[
            pl.BlockSpec((ROWS, width), lambda i, _: (i, 0)),
            pl.BlockSpec((ROWS, heads), lambda i, _: (i, 0)),
            pl.BlockSpec((heads, SPAN), lambda i, _: (0, 0)),
            pl.BlockSpec(qkv.shape, lambda i, _: (0, 0), pipeline_mode=pl.Buffered(1)),
            pl.BlockSpec(w.shape, lambda i, _: (0, 0), pipeline_mode=pl.Buffered(1)),
        ],
        out_specs=pl.BlockSpec((ROWS, width), lambda i, _: (i, 0)),
    )
    return pl.pallas_call(
        lambda *refs: retention_kernel(dims, *refs),
        grid_spec=grid_spec,
        out_shape=jax.ShapeDtypeStruct((SPAN, width), BF),
        compiler_params=pltpu.CompilerParams(vmem_limit_bytes=48 * 2**20),
        cost_estimate=pl.CostEstimate(flops=12 * 10**9, bytes_accessed=20 * 10**6, transcendentals=2 * 10**6),
        name="retention",
    )(scalars, x, running, running.T, qkv, w)


def ffn_kernel(scalars, x_ref, w_ref, *refs):
    out_ref = refs[-1]
    width = out_ref.shape[1]
    x = x_ref[...]
    gate = jnp.dot(x, w_ref[:, :width], preferred_element_type=F32)
    up = jnp.dot(x, w_ref[:, width:], preferred_element_type=F32)
    out_ref[...] = (gate / (1.0 + jnp.exp(-gate)) * up).astype(BF)


def ffn(x, place, w, held):
    rows, width = x.shape
    out_width = w.shape[1] // 2
    extra = [] if held is None else [held]
    grid_spec = pltpu.PrefetchScalarGridSpec(
        num_scalar_prefetch=1,
        grid=(1,),
        in_specs=[pl.BlockSpec((rows, width), lambda i, s: (0, 0)), pl.BlockSpec(w.shape, lambda i, s: (0, 0))]
        + [pl.BlockSpec(memory_space=pl.ANY)] * len(extra),
        out_specs=pl.BlockSpec((rows, out_width), lambda i, s: (s[0], 0)),
    )
    return pl.pallas_call(
        ffn_kernel,
        grid_spec=grid_spec,
        out_shape=jax.ShapeDtypeStruct((SPAN, out_width), BF),
        input_output_aliases={3: 0} if extra else {},
        compiler_params=pltpu.CompilerParams(vmem_limit_bytes=40 * 2**20),
        cost_estimate=pl.CostEstimate(
            flops=2 * rows * width * w.shape[1], bytes_accessed=2 * w.size, transcendentals=rows * out_width
        ),
        name="ffn",
    )(place.reshape(1).astype(jnp.int32), x, w, *extra)


def per_device(
    tokens, norm_gain, mlp_gain, lengths, log_decay,
    query_master, key_master, value_master, swish_master, output_master, ffn_gate_master, ffn_up_master,
):
    mp_count = lax.axis_size("mp")
    mp_index = lax.axis_index("mp")
    share = max(1, mp_count // H)
    heads = max(1, H // mp_count)

    def at_owner(parts):
        block = jnp.concatenate(parts, axis=2)
        block = lax.all_to_all(block, "mp", split_axis=0, concat_axis=0, tiled=True)
        return block.reshape(-1, block.shape[2])

    angles = jnp.arange(SPAN, dtype=jnp.int32).astype(F32)[:, None] * jnp.exp(
        (2 * jnp.arange(HALF, dtype=jnp.int32)).astype(F32) * (-math.log(10000.0) / DK)
    )
    cos, sin = jnp.cos(angles), jnp.sin(angles)
    first_head = mp_index // share * heads
    running = jnp.cumsum(lax.dynamic_slice_in_dim(log_decay, first_head, heads, 1), axis=0)

    qkv_rows = at_owner(
        [
            by_owner(even_odd(query_master.astype(BF)), DK, share, mp_count),
            by_owner(even_odd(key_master.astype(BF)), DK, share, mp_count),
            by_owner(value_master.astype(BF), DV, share, mp_count),
        ]
    )
    w_qkv = lax.all_gather(qkv_rows, "dp", axis=0, tiled=True)
    swish, output, qkv_rows = lax.optimization_barrier((swish_master, output_master, qkv_rows))
    gate_out_rows = at_owner(
        [by_owner(swish.astype(BF), DV, 1, mp_count), by_owner(output.astype(BF).T, DV, 1, mp_count)]
    )
    w_gate_out = lax.all_gather(gate_out_rows, "dp", axis=0, tiled=True)

    order = [(i, (i + 1) % mp_count) for i in range(mp_count)]
    moving, _ = lax.optimization_barrier((tokens, gate_out_rows))
    blocks, qkv = [moving], None
    for step in range(mp_count):
        if step < mp_count - 1:
            arriving = lax.ppermute(moving, "mp", order)
            blocks.append(arriving)
        if step > 0:
            qkv = project(blocks[step - 1], (mp_index - step + 1) % mp_count, norm_gain, cos, sin, w_qkv, heads, qkv)
        if step < mp_count - 1:
            moving = arriving
            if step > 0:
                moving, qkv = lax.optimization_barrier((moving, qkv))
    qkv = project(blocks[-1], (mp_index + 1) % mp_count, norm_gain, cos, sin, w_qkv, heads, qkv)
    ffn_parts, qkv = lax.optimization_barrier(((ffn_gate_master, ffn_up_master), qkv))
    ffn_pieces = exchanged(
        jnp.concatenate([by_owner(m.astype(BF), DV, 1, mp_count) for m in ffn_parts], axis=2), mp_index, mp_count
    )
    branch = retention(qkv[0], running, lengths[0], mp_index % share, qkv[1], w_gate_out, heads, share)
    ffn_pieces, branch = lax.optimization_barrier((ffn_pieces, branch))
    w_ffn = lax.all_gather(in_order(ffn_pieces, mp_index), "dp", axis=0, tiled=True)
    residual = (tokens.astype(F32) + ring_sum(branch, mp_index, mp_count)).astype(BF)
    moving = rms_rows(residual, mlp_gain)
    hidden = None
    for step in range(mp_count):
        block = moving
        if step < mp_count - 1:
            arriving = lax.ppermute(moving, "mp", order)
        hidden = ffn(block, (mp_index - step) % mp_count, w_ffn, hidden)
        if step < mp_count - 1:
            moving, hidden = lax.optimization_barrier((arriving, hidden))
    return residual, hidden


def solution(mesh):
    rows, columns = P(("dp", "mp"), None), P(None, ("dp", "mp"))
    placed = (rows, P(), P(), P("dp"), P("dp", None), rows, rows, rows, rows, columns, rows, rows)
    return jax.shard_map(
        per_device, mesh=mesh, in_specs=placed, out_specs=(rows, P("dp", "mp")), check_vma=False
    )
```

```python
import functools
import math

import jax
import jax.numpy as jnp
from jax import lax
from jax.experimental import pallas as pl
from jax.experimental.pallas import tpu as pltpu
from jax.sharding import PartitionSpec as P

H = 8
DK = 256
DV = 512
SPAN = 1024
HALF = DK // 2
BF = jnp.bfloat16
F32 = jnp.float32
STREAMS = 2


def rms_rows(row_block, gain_vec):
    values = row_block.astype(F32)
    scale = lax.rsqrt(jnp.mean(values * values, axis=-1, keepdims=True) + 1e-06)
    return (values * scale * gain_vec).astype(BF)


def even_odd(matrix):
    rows = matrix.shape[0]
    new = jnp.arange(DK, dtype=jnp.int32)
    old = jnp.where(new < HALF, 2 * new, 2 * (new - HALF) + 1)
    one_hot = (jnp.arange(DK, dtype=jnp.int32)[:, None] == old[None, :]).astype(BF)
    heads = matrix.reshape(rows * H, DK)
    return jnp.dot(heads, one_hot, preferred_element_type=F32).astype(BF).reshape(rows, H * DK)


def by_owner(matrix, width, share, mp_count):
    rows = matrix.shape[0]
    if share > 1:
        heads = jnp.repeat(matrix.reshape(rows, H, width), share, axis=1)
        return heads.transpose(1, 0, 2)
    return matrix.reshape(rows, mp_count, -1).transpose(1, 0, 2)


def assemble_kernel(scalars, *refs):
    pieces, out_ref = refs[:-1], refs[-1]
    rows = pieces[0].shape[0]
    for step, piece in enumerate(pieces):
        place = lax.rem(scalars[0] - step + len(pieces), len(pieces))
        out_ref[pl.ds(pl.multiple_of(place * rows, rows), rows), :] = piece[...]


def in_order(pieces, index):
    rows, width = pieces[0].shape
    grid_spec = pltpu.PrefetchScalarGridSpec(
        num_scalar_prefetch=1,
        grid=(1,),
        in_specs=[pl.BlockSpec((rows, width), lambda i, s: (0, 0))] * len(pieces),
        out_specs=pl.BlockSpec((rows * len(pieces), width), lambda i, s: (0, 0)),
    )
    return pl.pallas_call(
        assemble_kernel,
        grid_spec=grid_spec,
        out_shape=jax.ShapeDtypeStruct((rows * len(pieces), width), BF),
        compiler_params=pltpu.CompilerParams(vmem_limit_bytes=16 * 2**20),
        name="assemble",
    )(index.reshape(1).astype(jnp.int32), *pieces)


def exchanged(block, index, count):
    pieces = []
    for shift in range(count):
        piece = lax.dynamic_index_in_dim(block, (index + shift) % count, 0, keepdims=False)
        if shift:
            piece = lax.ppermute(piece, "mp", [(i, (i + shift) % count) for i in range(count)])
        pieces.append(piece)
    return pieces


def stacked(refs):
    return jnp.concatenate([ref[...] for ref in refs], axis=0)


def project_kernel(heads, scalars, *refs):
    halves, (gain_ref, cos_ref, sin_ref, w_ref, normed_ref, out_ref) = refs[:-6], refs[-6:]
    wq = heads * DK
    x = rms_rows(stacked(halves), gain_ref[...])
    normed_ref[...] = x
    cos, sin = cos_ref[...], sin_ref[...]
    for h in range(2 * heads):
        low = h * DK
        both = jnp.dot(x, w_ref[:, low : low + DK], preferred_element_type=F32)
        a, b = both[:, :HALF], both[:, HALF:]
        scale = DK**-0.5 if h < heads else 1.0
        out_ref[:, low : low + HALF] = ((a * cos - b * sin) * scale).astype(BF)
        out_ref[:, low + HALF : low + DK] = ((b * cos + a * sin) * scale).astype(BF)
    out_ref[:, 2 * wq :] = jnp.dot(x, w_ref[:, 2 * wq :], preferred_element_type=F32).astype(BF)


def project(halves, place, gain, cos, sin, w, heads):
    half, width = halves[0].shape
    rows = half * len(halves)
    out_width = w.shape[1]
    grid_spec = pltpu.PrefetchScalarGridSpec(
        num_scalar_prefetch=1,
        grid=(1,),
        in_specs=[pl.BlockSpec((half, width), lambda i, s: (0, 0))] * len(halves)
        + [
            pl.BlockSpec((1, width), lambda i, s: (0, 0)),
            pl.BlockSpec((rows, HALF), lambda i, s: (s[0], 0)),
            pl.BlockSpec((rows, HALF), lambda i, s: (s[0], 0)),
            pl.BlockSpec(w.shape, lambda i, s: (0, 0), pipeline_mode=pl.Buffered(1)),
        ],
        out_specs=[
            pl.BlockSpec((rows, width), lambda i, s: (0, 0)),
            pl.BlockSpec((rows, out_width), lambda i, s: (0, 0)),
        ],
    )
    return pl.pallas_call(
        lambda *refs: project_kernel(heads, *refs),
        grid_spec=grid_spec,
        out_shape=[jax.ShapeDtypeStruct((rows, width), BF), jax.ShapeDtypeStruct((rows, out_width), BF)],
        compiler_params=pltpu.CompilerParams(vmem_limit_bytes=20 * 2**20),
        cost_estimate=pl.CostEstimate(flops=rows * width * out_width // 2, bytes_accessed=2**20, transcendentals=0),
        name="project",
    )(place.reshape(1).astype(jnp.int32), *halves, gain.reshape(1, -1), cos, sin, w)


def retention_kernel(dims, scalars, x_ref, run_col, run_row, *refs):
    heads, share, wq, wv, wg, count, own = dims
    blocks = refs[:count]
    w_hbm, out_refs = refs[count], refs[count + 1 : -4]
    kept_ref, wg_ref, wo_ref, arrived = refs[-4:]
    gate_copy = pltpu.make_async_copy(w_hbm.at[:, :wg], wg_ref, arrived.at[0])
    out_copy = pltpu.make_async_copy(w_hbm.at[:, wg:], wo_ref, arrived.at[1])
    gate_copy.start()
    out_copy.start()
    rows = x_ref.shape[0]
    device = scalars[2]
    block = lax.rem(device - own + count, count)
    live = block * rows + lax.broadcasted_iota(jnp.int32, (rows, 1), 0) < scalars[0]

    def add(past, held, first):
        for h in range(heads):
            scores = lax.dot_general(
                blocks[own][:, h * DK : (h + 1) * DK],
                blocks[past][:, wq + h * DK : wq + (h + 1) * DK],
                (((1,), (1,)), ((), ())),
                preferred_element_type=F32,
            )
            gap = run_col[:, h : h + 1] - run_row[held, h : h + 1, :]
            if first:
                t = lax.broadcasted_iota(jnp.int32, (rows, rows), 0)
                s = lax.broadcasted_iota(jnp.int32, (rows, rows), 1)
                gap = jnp.where(t >= s, gap, -jnp.inf)
            weights = (scores * jnp.exp(gap)).astype(BF)
            values = blocks[past][:, 2 * wq + h * DV : 2 * wq + (h + 1) * DV]
            more = jnp.dot(weights, values, preferred_element_type=F32)
            place = slice(h * DV, (h + 1) * DV)
            kept_ref[:, place] = more if first else kept_ref[:, place] + more

    add(own, block, True)
    for past in range(count):
        held = lax.rem(device - past + count, count)
        if past != own:
            pl.when(held < block)(functools.partial(add, past, held, False))

    pieces = []
    for h in range(heads):
        kept = kept_ref[:, h * DV : (h + 1) * DV]
        mean = jnp.mean(kept, axis=-1, keepdims=True)
        spread = jnp.mean(kept * kept, axis=-1, keepdims=True) - mean * mean
        normed = (kept - mean) * lax.rsqrt(spread + 1e-05)
        if share > 1:
            mine = normed[:, :wg]
            for bit in range(1, share):
                mine = jnp.where(scalars[1] == bit, normed[:, bit * wg : (bit + 1) * wg], mine)
            normed = mine
        pieces.append(normed)
    whole = jnp.concatenate(pieces, axis=1) if heads > 1 else pieces[0]
    gate_copy.wait()
    gate = jnp.dot(x_ref[...], wg_ref[...], preferred_element_type=F32).astype(BF).astype(F32)
    gate = gate / (1.0 + jnp.exp(-gate))
    gated = jnp.where(live, gate * whole, 0.0).astype(BF)
    out_copy.wait()
    half = rows // len(out_refs)
    for k, out_ref in enumerate(out_refs):
        out_ref[...] = lax.dot_general(
            gated[k * half : (k + 1) * half], wo_ref[...], (((1,), (1,)), ((), ())), preferred_element_type=F32
        ).astype(BF)


def retention(own, index, x, running, length, partner, blocks, w, heads, share):
    count, (rows, width) = len(blocks), x.shape
    wq, wv, wg = heads * DK, heads * DV, w.shape[1] // 2
    dims = (heads, share, wq, wv, wg, count, own)
    scalars = jnp.stack([length, partner, index]).astype(jnp.int32)
    w = pltpu.with_memory_space_constraint(w, pltpu.HBM)
    by_row = running.T.reshape(heads, count, rows).transpose(1, 0, 2)
    grid_spec = pltpu.PrefetchScalarGridSpec(
        num_scalar_prefetch=1,
        grid=(1,),
        in_specs=[
            pl.BlockSpec((rows, width), lambda i, s: (0, 0)),
            pl.BlockSpec((rows, heads), lambda i, s: (lax.rem(s[2] - own + count, count), 0)),
            pl.BlockSpec(by_row.shape, lambda i, s: (0, 0, 0)),
        ]
        + [pl.BlockSpec(blocks[0].shape, lambda i, s: (0, 0), pipeline_mode=pl.Buffered(1))] * count
        + [pl.BlockSpec(memory_space=pl.ANY)],
        out_specs=[pl.BlockSpec((rows // STREAMS, width), lambda i, s: (0, 0))] * STREAMS,
        scratch_shapes=[
            pltpu.VMEM((rows, wv), F32),
            pltpu.VMEM((width, wg), BF),
            pltpu.VMEM((width, wg), BF),
            pltpu.SemaphoreType.DMA((2,)),
        ],
    )
    return pl.pallas_call(
        lambda *refs: retention_kernel(dims, *refs),
        grid_spec=grid_spec,
        out_shape=[jax.ShapeDtypeStruct((rows // STREAMS, width), BF)] * STREAMS,
        compiler_params=pltpu.CompilerParams(vmem_limit_bytes=22 * 2**20),
        cost_estimate=pl.CostEstimate(flops=3 * 10**9, bytes_accessed=2**20, transcendentals=10**5),
        name="retention",
    )(scalars, x, running, by_row, *blocks, w)


def middle_kernel(came_ref, part_ref, token_ref, gain_ref, residual_ref, normed_ref):
    branch = came_ref[...].astype(F32) + part_ref[...].astype(F32)
    residual_ref[...] = (token_ref[...].astype(F32) + branch).astype(BF)
    normed_ref[...] = rms_rows(residual_ref[...], gain_ref[...])


def middle(came, part, tokens, gain):
    rows, width = tokens.shape
    step = min(rows, 64)
    block = pl.BlockSpec((step, width), lambda i: (i, 0))
    return pl.pallas_call(
        middle_kernel,
        grid=(rows // step,),
        in_specs=[block, block, block, pl.BlockSpec((1, width), lambda i: (0, 0))],
        out_specs=[block, block],
        out_shape=[jax.ShapeDtypeStruct((rows, width), BF)] * 2,
        compiler_params=pltpu.CompilerParams(vmem_limit_bytes=16 * 2**20),
        name="middle",
    )(came, part, tokens, gain.reshape(1, -1))


def ffn_kernel(count, scalars, *refs):
    w_ref, out_ref = refs[count], refs[-1]
    width = out_ref.shape[1]
    x = stacked(refs[:count])
    gate = jnp.dot(x, w_ref[:, :width], preferred_element_type=F32)
    up = jnp.dot(x, w_ref[:, width:], preferred_element_type=F32)
    out_ref[...] = (gate / (1.0 + jnp.exp(-gate)) * up).astype(BF)


def ffn(halves, place, w, held):
    half, width = halves[0].shape
    rows = half * len(halves)
    out_width = w.shape[1] // 2
    extra = [] if held is None else [held]
    grid_spec = pltpu.PrefetchScalarGridSpec(
        num_scalar_prefetch=1,
        grid=(1,),
        in_specs=[pl.BlockSpec((half, width), lambda i, s: (0, 0))] * len(halves)
        + [pl.BlockSpec(w.shape, lambda i, s: (0, 0))]
        + [pl.BlockSpec(memory_space=pl.ANY)] * len(extra),
        out_specs=pl.BlockSpec((rows, out_width), lambda i, s: (s[0], 0)),
    )
    return pl.pallas_call(
        lambda *refs: ffn_kernel(len(halves), *refs),
        grid_spec=grid_spec,
        out_shape=jax.ShapeDtypeStruct((SPAN, out_width), BF),
        input_output_aliases={len(halves) + 2: 0} if extra else {},
        compiler_params=pltpu.CompilerParams(vmem_limit_bytes=18 * 2**20),
        cost_estimate=pl.CostEstimate(
            flops=2 * rows * width * w.shape[1], bytes_accessed=2 * w.size, transcendentals=rows * out_width
        ),
        name="ffn",
    )(place.reshape(1).astype(jnp.int32), *halves, w, *extra)


def per_device(
    tokens, norm_gain, mlp_gain, lengths, log_decay,
    query_master, key_master, value_master, swish_master, output_master, ffn_gate_master, ffn_up_master,
):
    mp_count = lax.axis_size("mp")
    mp_index = lax.axis_index("mp")
    share = max(1, mp_count // H)
    heads = max(1, H // mp_count)

    angles = jnp.arange(SPAN, dtype=jnp.int32).astype(F32)[:, None] * jnp.exp(
        (2 * jnp.arange(HALF, dtype=jnp.int32)).astype(F32) * (-math.log(10000.0) / DK)
    )
    cos, sin = jnp.cos(angles), jnp.sin(angles)
    first_head = mp_index // share * heads
    running = jnp.cumsum(lax.dynamic_slice_in_dim(log_decay, first_head, heads, 1), axis=0)

    qkv_pieces = exchanged(
        jnp.concatenate(
            [
                by_owner(even_odd(query_master.astype(BF)), DK, share, mp_count),
                by_owner(even_odd(key_master.astype(BF)), DK, share, mp_count),
                by_owner(value_master.astype(BF), DV, share, mp_count),
            ],
            axis=2,
        ),
        mp_index,
        mp_count,
    )
    gate_out_block = jnp.concatenate(
        [by_owner(swish_master.astype(BF), DV, 1, mp_count), by_owner(output_master.astype(BF).T, DV, 1, mp_count)],
        axis=2,
    )
    gate_out_block, qkv_pieces = lax.optimization_barrier((gate_out_block, qkv_pieces))
    gate_out_pieces = exchanged(gate_out_block, mp_index, mp_count)
    qkv_rows = in_order(qkv_pieces, mp_index)
    w_qkv = lax.all_gather(qkv_rows, "dp", axis=0, tiled=True)

    order = [(i, (i + 1) % mp_count) for i in range(mp_count)]

    def onward(halves):
        return [lax.ppermute(half, "mp", order) for half in halves]

    def projected(step):
        return project(blocks[step], (mp_index - step) % mp_count, norm_gain, cos, sin, w_qkv, heads)

    def held_back(later, *first):
        return lax.optimization_barrier((later, first))[0]

    half = tokens.shape[0] // STREAMS
    token_halves = [tokens[k * half : (k + 1) * half] for k in range(STREAMS)]
    masters = held_back((ffn_gate_master, ffn_up_master), qkv_rows)
    ffn_block = jnp.concatenate([by_owner(m.astype(BF), DV, 1, mp_count) for m in masters], axis=2)
    blocks, done = [held_back(token_halves, qkv_rows)], []
    for step in range(1, mp_count):
        blocks.append(onward(blocks[-1]))
        if step == 1:
            blocks[1] = [held_back(h, ffn_block) for h in blocks[1]]
        else:
            done.append(projected(step - 2))
            if step < mp_count - 1:
                blocks[step] = [held_back(h, done[-1]) for h in blocks[step]]
            if step == 2:
                gate_out_pieces = held_back(gate_out_pieces, blocks[1])
                w_gate_out = lax.all_gather(in_order(gate_out_pieces, mp_index), "dp", axis=0, tiled=True)
    done.append(projected(mp_count - 2))
    ffn_block, blocks[-1] = held_back((ffn_block, blocks[-1]), done, blocks[-1])
    ffn_pieces = exchanged(ffn_block, mp_index, mp_count)
    done.append(projected(mp_count - 1))
    normed, qkv = [d[0] for d in done], [d[1] for d in done]

    for step in range(mp_count):
        own = (1 + step) % mp_count
        parts = retention(
            own, mp_index, normed[own], running, lengths[0], mp_index % share, qkv, w_gate_out, heads, share
        )
        if step < mp_count - 1:
            later = (2 + step) % mp_count
            normed[later] = held_back(normed[later], parts)
        if step == 0:
            ffn_pieces = held_back(ffn_pieces, parts)
            w_ffn = lax.all_gather(in_order(ffn_pieces, mp_index), "dp", axis=0, tiled=True)
            totals = parts
        elif step < mp_count - 1:
            totals = [(c.astype(F32) + p.astype(F32)).astype(BF) for c, p in zip(came, parts)]
        if step < mp_count - 1:
            came = onward(totals)
    finished = [middle(c, p, t, mlp_gain) for c, p, t in zip(came, parts, token_halves)]
    residual = jnp.concatenate([f[0] for f in finished], axis=0)
    moving = [f[1] for f in finished]
    hidden = None
    for step in range(mp_count):
        here = moving
        if step < mp_count - 1:
            arriving = onward(moving)
        hidden = ffn(here, (mp_index - step) % mp_count, w_ffn, hidden)
        if step < mp_count - 1:
            moving = [held_back(h, hidden) for h in arriving] if step else arriving
    return residual, hidden


def solution(mesh):
    rows, columns = P(("dp", "mp"), None), P(None, ("dp", "mp"))
    placed = (rows, P(), P(), P("dp"), P("dp", None), rows, rows, rows, rows, columns, rows, rows)
    return jax.shard_map(
        per_device, mesh=mesh, in_specs=placed, out_specs=(rows, P("dp", "mp")), check_vma=False
    )
```

```python
import functools
import math

import jax
import jax.numpy as jnp
from jax import lax
from jax.experimental import pallas as pl
from jax.experimental.pallas import tpu as pltpu
from jax.sharding import PartitionSpec as P

H = 8
DK = 256
DV = 512
SPAN = 1024
HALF = DK // 2
BF = jnp.bfloat16
F32 = jnp.float32
STREAMS = 2
CHUNK = 256


def rms_rows(row_block, gain_vec):
    values = row_block.astype(F32)
    scale = lax.rsqrt(jnp.mean(values * values, axis=-1, keepdims=True) + 1e-06)
    return (values * scale * gain_vec).astype(BF)


def even_odd(matrix):
    rows = matrix.shape[0]
    new = jnp.arange(DK, dtype=jnp.int32)
    old = jnp.where(new < HALF, 2 * new, 2 * (new - HALF) + 1)
    one_hot = (jnp.arange(DK, dtype=jnp.int32)[:, None] == old[None, :]).astype(BF)
    heads = matrix.reshape(rows * H, DK)
    return jnp.dot(heads, one_hot, preferred_element_type=F32).astype(BF).reshape(rows, H * DK)


def by_owner(matrix, width, share, mp_count):
    rows = matrix.shape[0]
    if share > 1:
        heads = jnp.repeat(matrix.reshape(rows, H, width), share, axis=1)
        return heads.transpose(1, 0, 2)
    return matrix.reshape(rows, mp_count, -1).transpose(1, 0, 2)


def assemble_kernel(scalars, *refs):
    pieces, out_ref = refs[:-1], refs[-1]
    rows = pieces[0].shape[0]
    for step, piece in enumerate(pieces):
        place = lax.rem(scalars[0] - step + len(pieces), len(pieces))
        out_ref[pl.ds(pl.multiple_of(place * rows, rows), rows), :] = piece[...]


def in_order(pieces, index):
    rows, width = pieces[0].shape
    grid_spec = pltpu.PrefetchScalarGridSpec(
        num_scalar_prefetch=1,
        grid=(1,),
        in_specs=[pl.BlockSpec((rows, width), lambda i, s: (0, 0))] * len(pieces),
        out_specs=pl.BlockSpec((rows * len(pieces), width), lambda i, s: (0, 0)),
    )
    return pl.pallas_call(
        assemble_kernel,
        grid_spec=grid_spec,
        out_shape=jax.ShapeDtypeStruct((rows * len(pieces), width), BF),
        compiler_params=pltpu.CompilerParams(vmem_limit_bytes=16 * 2**20),
        name="assemble",
    )(index.reshape(1).astype(jnp.int32), *pieces)


def exchanged(block, index, count):
    pieces = []
    for shift in range(count):
        piece = lax.dynamic_index_in_dim(block, (index + shift) % count, 0, keepdims=False)
        if shift:
            piece = lax.ppermute(piece, "mp", [(i, (i + shift) % count) for i in range(count)])
        pieces.append(piece)
    return pieces


def stacked(refs):
    return jnp.concatenate([ref[...] for ref in refs], axis=0)


def chunk(i):
    return pl.ds(pl.multiple_of(i * CHUNK, CHUNK), CHUNK)


def project_kernel(heads, scalars, *refs):
    halves, (gain_ref, cos_ref, sin_ref, w_ref, normed_ref, out_ref) = refs[:-6], refs[-6:]
    wq = heads * DK
    normed_ref[...] = rms_rows(stacked(halves), gain_ref[...])

    def turn(h, _):
        both = jnp.dot(normed_ref[...], w_ref[:, chunk(h)], preferred_element_type=F32)
        a, b = both[:, :HALF], both[:, HALF:]
        cos, sin = cos_ref[...], sin_ref[...]
        scale = jnp.where(h < heads, DK**-0.5, 1.0)
        out_ref[:, pl.ds(pl.multiple_of(h * DK, DK), HALF)] = ((a * cos - b * sin) * scale).astype(BF)
        out_ref[:, pl.ds(pl.multiple_of(h * DK + HALF, HALF), HALF)] = ((b * cos + a * sin) * scale).astype(BF)
        return _

    def plain(i, _):
        out_ref[:, chunk(i)] = jnp.dot(normed_ref[...], w_ref[:, chunk(i)], preferred_element_type=F32).astype(BF)
        return _

    lax.fori_loop(0, 2 * heads, turn, 0)
    lax.fori_loop(2 * wq // CHUNK, out_ref.shape[1] // CHUNK, plain, 0)


def project(halves, place, gain, cos, sin, w, heads):
    half, width = halves[0].shape
    rows = half * len(halves)
    out_width = w.shape[1]
    grid_spec = pltpu.PrefetchScalarGridSpec(
        num_scalar_prefetch=1,
        grid=(1,),
        in_specs=[pl.BlockSpec((half, width), lambda i, s: (0, 0))] * len(halves)
        + [
            pl.BlockSpec((1, width), lambda i, s: (0, 0)),
            pl.BlockSpec((rows, HALF), lambda i, s: (s[0], 0)),
            pl.BlockSpec((rows, HALF), lambda i, s: (s[0], 0)),
            pl.BlockSpec(w.shape, lambda i, s: (0, 0), pipeline_mode=pl.Buffered(1)),
        ],
        out_specs=[
            pl.BlockSpec((rows, width), lambda i, s: (0, 0)),
            pl.BlockSpec((rows, out_width), lambda i, s: (0, 0)),
        ],
    )
    return pl.pallas_call(
        lambda *refs: project_kernel(heads, *refs),
        grid_spec=grid_spec,
        out_shape=[jax.ShapeDtypeStruct((rows, width), BF), jax.ShapeDtypeStruct((rows, out_width), BF)],
        compiler_params=pltpu.CompilerParams(vmem_limit_bytes=20 * 2**20),
        cost_estimate=pl.CostEstimate(flops=rows * width * out_width // 2, bytes_accessed=2**20, transcendentals=0),
        name="project",
    )(place.reshape(1).astype(jnp.int32), *halves, gain.reshape(1, -1), cos, sin, w)


def retention_kernel(dims, scalars, run_col, run_row, x_hbm, *refs):
    heads, share, wq, wv, wg, count, own = dims
    blocks, w_hbm, out_refs = refs[:count], refs[count], refs[count + 1 : -7]
    held_ref, x_ref, kept_ref, gated_ref, wg_ref, wo_ref, arrived = refs[-7:]
    rows, width = x_ref.shape
    order = [own] + [k for k in range(count) if k != own]
    copies = [pltpu.make_async_copy(blocks[k], held_ref.at[k], arrived.at[k]) for k in order]
    copies += [
        pltpu.make_async_copy(x_hbm, x_ref, arrived.at[count]),
        pltpu.make_async_copy(w_hbm.at[:, :wg], wg_ref, arrived.at[count + 1]),
        pltpu.make_async_copy(w_hbm.at[:, wg:], wo_ref, arrived.at[count + 2]),
    ]
    for copy in copies:
        copy.start()
    device = scalars[2]
    block = lax.rem(device - own + count, count)
    live = block * rows + lax.broadcasted_iota(jnp.int32, (rows, 1), 0) < scalars[0]

    def add(past, held, first):
        for h in range(heads):
            scores = lax.dot_general(
                held_ref[own, :, h * DK : (h + 1) * DK],
                held_ref[past, :, wq + h * DK : wq + (h + 1) * DK],
                (((1,), (1,)), ((), ())),
                preferred_element_type=F32,
            )
            gap = run_col[:, h : h + 1] - run_row[held, h : h + 1, :]
            if first:
                t = lax.broadcasted_iota(jnp.int32, (rows, rows), 0)
                s = lax.broadcasted_iota(jnp.int32, (rows, rows), 1)
                gap = jnp.where(t >= s, gap, -jnp.inf)
            weights = (scores * jnp.exp(gap)).astype(BF)
            values = held_ref[past, :, 2 * wq + h * DV : 2 * wq + (h + 1) * DV]
            more = jnp.dot(weights, values, preferred_element_type=F32)
            place = slice(h * DV, (h + 1) * DV)
            kept_ref[:, place] = more if first else kept_ref[:, place] + more

    copies[0].wait()
    add(own, block, True)
    for copy in copies[1:count]:
        copy.wait()

    def earlier(held, _):
        add(lax.rem(device - held + count, count), held, False)
        return _

    lax.fori_loop(0, block, earlier, 0)

    for h in range(heads):
        kept = kept_ref[:, h * DV : (h + 1) * DV]
        mean = jnp.mean(kept, axis=-1, keepdims=True)
        spread = jnp.mean(kept * kept, axis=-1, keepdims=True) - mean * mean
        normed = (kept - mean) * lax.rsqrt(spread + 1e-05)
        if share > 1:
            mine = normed[:, :wg]
            for bit in range(1, share):
                mine = jnp.where(scalars[1] == bit, normed[:, bit * wg : (bit + 1) * wg], mine)
            kept_ref[:, :wg] = mine
        else:
            kept_ref[:, h * DV : (h + 1) * DV] = normed

    copies[count].wait()
    copies[count + 1].wait()

    def gating(i, _):
        gate = jnp.dot(x_ref[...], wg_ref[:, chunk(i)], preferred_element_type=F32).astype(BF).astype(F32)
        gate = gate / (1.0 + jnp.exp(-gate))
        gated_ref[:, chunk(i)] = jnp.where(live, gate * kept_ref[:, chunk(i)], 0.0).astype(BF)
        return _

    lax.fori_loop(0, wg // CHUNK, gating, 0)
    copies[count + 2].wait()
    half = rows // len(out_refs)

    def leaving(i, _):
        branch = lax.dot_general(
            gated_ref[...], wo_ref[chunk(i), :], (((1,), (1,)), ((), ())), preferred_element_type=F32
        ).astype(BF)
        for k, out_ref in enumerate(out_refs):
            out_ref[:, chunk(i)] = branch[k * half : (k + 1) * half]
        return _

    lax.fori_loop(0, width // CHUNK, leaving, 0)


def retention(own, index, x, running, length, partner, blocks, w, heads, share):
    count, (rows, width) = len(blocks), x.shape
    wq, wv, wg = heads * DK, heads * DV, w.shape[1] // 2
    dims = (heads, share, wq, wv, wg, count, own)
    scalars = jnp.stack([length, partner, index]).astype(jnp.int32)
    x, w, *blocks = [pltpu.with_memory_space_constraint(a, pltpu.HBM) for a in (x, w, *blocks)]
    by_row = running.T.reshape(heads, count, rows).transpose(1, 0, 2)
    grid_spec = pltpu.PrefetchScalarGridSpec(
        num_scalar_prefetch=1,
        grid=(1,),
        in_specs=[
            pl.BlockSpec((rows, heads), lambda i, s: (lax.rem(s[2] - own + count, count), 0)),
            pl.BlockSpec(by_row.shape, lambda i, s: (0, 0, 0)),
        ]
        + [pl.BlockSpec(memory_space=pl.ANY)] * (count + 2),
        out_specs=[pl.BlockSpec((rows // STREAMS, width), lambda i, s: (0, 0))] * STREAMS,
        scratch_shapes=[
            pltpu.VMEM((count, *blocks[0].shape), BF),
            pltpu.VMEM((rows, width), BF),
            pltpu.VMEM((rows, wv), F32),
            pltpu.VMEM((rows, wg), BF),
            pltpu.VMEM((width, wg), BF),
            pltpu.VMEM((width, wg), BF),
            pltpu.SemaphoreType.DMA((count + 3,)),
        ],
    )
    return pl.pallas_call(
        lambda *refs: retention_kernel(dims, *refs),
        grid_spec=grid_spec,
        out_shape=[jax.ShapeDtypeStruct((rows // STREAMS, width), BF)] * STREAMS,
        compiler_params=pltpu.CompilerParams(vmem_limit_bytes=24 * 2**20),
        cost_estimate=pl.CostEstimate(flops=3 * 10**9, bytes_accessed=2**20, transcendentals=10**5),
        name="retention",
    )(scalars, running, by_row, x, *blocks, w)


def middle_kernel(came_ref, part_ref, token_ref, gain_ref, residual_ref, normed_ref):
    branch = came_ref[...].astype(F32) + part_ref[...].astype(F32)
    residual_ref[...] = (token_ref[...].astype(F32) + branch).astype(BF)
    normed_ref[...] = rms_rows(residual_ref[...], gain_ref[...])


def middle(came, part, tokens, gain):
    rows, width = tokens.shape
    step = min(rows, 64)
    block = pl.BlockSpec((step, width), lambda i: (i, 0))
    return pl.pallas_call(
        middle_kernel,
        grid=(rows // step,),
        in_specs=[block, block, block, pl.BlockSpec((1, width), lambda i: (0, 0))],
        out_specs=[block, block],
        out_shape=[jax.ShapeDtypeStruct((rows, width), BF)] * 2,
        compiler_params=pltpu.CompilerParams(vmem_limit_bytes=16 * 2**20),
        name="middle",
    )(came, part, tokens, gain.reshape(1, -1))


def ffn_kernel(count, scalars, *refs):
    w_ref, out_ref, x_ref = refs[count], refs[-2], refs[-1]
    x_ref[...] = stacked(refs[:count])
    chunks = out_ref.shape[1] // CHUNK

    def one(i, _):
        gate = jnp.dot(x_ref[...], w_ref[:, chunk(i)], preferred_element_type=F32)
        up = jnp.dot(x_ref[...], w_ref[:, chunk(i + chunks)], preferred_element_type=F32)
        out_ref[:, chunk(i)] = (gate / (1.0 + jnp.exp(-gate)) * up).astype(BF)
        return _

    lax.fori_loop(0, chunks, one, 0)


def ffn(halves, place, w, held):
    half, width = halves[0].shape
    rows = half * len(halves)
    out_width = w.shape[1] // 2
    extra = [] if held is None else [held]
    grid_spec = pltpu.PrefetchScalarGridSpec(
        num_scalar_prefetch=1,
        grid=(1,),
        in_specs=[pl.BlockSpec((half, width), lambda i, s: (0, 0))] * len(halves)
        + [pl.BlockSpec(w.shape, lambda i, s: (0, 0))]
        + [pl.BlockSpec(memory_space=pl.ANY)] * len(extra),
        out_specs=pl.BlockSpec((rows, out_width), lambda i, s: (s[0], 0)),
        scratch_shapes=[pltpu.VMEM((rows, width), BF)],
    )
    return pl.pallas_call(
        lambda *refs: ffn_kernel(len(halves), *refs),
        grid_spec=grid_spec,
        out_shape=jax.ShapeDtypeStruct((SPAN, out_width), BF),
        input_output_aliases={len(halves) + 2: 0} if extra else {},
        compiler_params=pltpu.CompilerParams(vmem_limit_bytes=18 * 2**20),
        cost_estimate=pl.CostEstimate(
            flops=2 * rows * width * w.shape[1], bytes_accessed=2 * w.size, transcendentals=rows * out_width
        ),
        name="ffn",
    )(place.reshape(1).astype(jnp.int32), *halves, w, *extra)


def per_device(
    tokens, norm_gain, mlp_gain, lengths, log_decay,
    query_master, key_master, value_master, swish_master, output_master, ffn_gate_master, ffn_up_master,
):
    mp_count = lax.axis_size("mp")
    mp_index = lax.axis_index("mp")
    share = max(1, mp_count // H)
    heads = max(1, H // mp_count)

    angles = jnp.arange(SPAN, dtype=jnp.int32).astype(F32)[:, None] * jnp.exp(
        (2 * jnp.arange(HALF, dtype=jnp.int32)).astype(F32) * (-math.log(10000.0) / DK)
    )
    cos, sin = jnp.cos(angles), jnp.sin(angles)
    first_head = mp_index // share * heads
    running = jnp.cumsum(lax.dynamic_slice_in_dim(log_decay, first_head, heads, 1), axis=0)

    qkv_pieces = exchanged(
        jnp.concatenate(
            [
                by_owner(even_odd(query_master.astype(BF)), DK, share, mp_count),
                by_owner(even_odd(key_master.astype(BF)), DK, share, mp_count),
                by_owner(value_master.astype(BF), DV, share, mp_count),
            ],
            axis=2,
        ),
        mp_index,
        mp_count,
    )
    gate_out_block = jnp.concatenate(
        [by_owner(swish_master.astype(BF), DV, 1, mp_count), by_owner(output_master.astype(BF).T, DV, 1, mp_count)],
        axis=2,
    )
    gate_out_block, qkv_pieces = lax.optimization_barrier((gate_out_block, qkv_pieces))
    gate_out_pieces = exchanged(gate_out_block, mp_index, mp_count)
    qkv_rows = in_order(qkv_pieces, mp_index)
    w_qkv = lax.all_gather(qkv_rows, "dp", axis=0, tiled=True)

    order = [(i, (i + 1) % mp_count) for i in range(mp_count)]

    def onward(halves):
        return [lax.ppermute(half, "mp", order) for half in halves]

    def projected(step):
        return project(blocks[step], (mp_index - step) % mp_count, norm_gain, cos, sin, w_qkv, heads)

    def held_back(later, *first):
        return lax.optimization_barrier((later, first))[0]

    half = tokens.shape[0] // STREAMS
    token_halves = [tokens[k * half : (k + 1) * half] for k in range(STREAMS)]
    masters = held_back((ffn_gate_master, ffn_up_master), qkv_rows)
    ffn_block = jnp.concatenate([by_owner(m.astype(BF), DV, 1, mp_count) for m in masters], axis=2)
    blocks, done = [held_back(token_halves, qkv_rows)], []
    for step in range(1, mp_count):
        blocks.append(onward(blocks[-1]))
        if step == 1:
            blocks[1] = [held_back(h, ffn_block) for h in blocks[1]]
        else:
            done.append(projected(step - 2))
            if step < mp_count - 1:
                blocks[step] = [held_back(h, done[-1]) for h in blocks[step]]
            if step == 2:
                w_gate_out = lax.all_gather(in_order(gate_out_pieces, mp_index), "dp", axis=0, tiled=True)
    done.append(projected(mp_count - 2))
    ffn_block, blocks[-1] = held_back((ffn_block, blocks[-1]), done, blocks[-1])
    ffn_pieces = exchanged(ffn_block, mp_index, mp_count)
    done.append(projected(mp_count - 1))
    normed, qkv = [d[0] for d in done], [d[1] for d in done]

    for step in range(mp_count):
        own = (1 + step) % mp_count
        parts = retention(
            own, mp_index, normed[own], running, lengths[0], mp_index % share, qkv, w_gate_out, heads, share
        )
        if step < mp_count - 1:
            later = (2 + step) % mp_count
            normed[later] = held_back(normed[later], parts)
        if step == 0:
            ffn_pieces = held_back(ffn_pieces, parts)
            w_ffn = lax.all_gather(in_order(ffn_pieces, mp_index), "dp", axis=0, tiled=True)
            totals = parts
        elif step < mp_count - 1:
            totals = [(c.astype(F32) + p.astype(F32)).astype(BF) for c, p in zip(came, parts)]
        if step < mp_count - 1:
            came = onward(totals)
    finished = [middle(c, p, t, mlp_gain) for c, p, t in zip(came, parts, token_halves)]
    residual = jnp.concatenate([f[0] for f in finished], axis=0)
    moving = [f[1] for f in finished]
    hidden = None
    for step in range(mp_count):
        here = moving
        if step < mp_count - 1:
            arriving = onward(moving)
        hidden = ffn(here, (mp_index - step) % mp_count, w_ffn, hidden)
        if step < mp_count - 1:
            moving = [held_back(h, hidden) for h in arriving] if step else arriving
    return residual, hidden


def solution(mesh):
    rows, columns = P(("dp", "mp"), None), P(None, ("dp", "mp"))
    placed = (rows, P(), P(), P("dp"), P("dp", None), rows, rows, rows, rows, columns, rows, rows)
    return jax.shard_map(
        per_device, mesh=mesh, in_specs=placed, out_specs=(rows, P("dp", "mp")), check_vma=False
    )
```

```python
import functools
import math

import jax
import jax.numpy as jnp
from jax import lax
from jax.experimental import pallas as pl
from jax.experimental.pallas import tpu as pltpu
from jax.sharding import PartitionSpec as P

H = 8
DK = 256
DV = 512
SPAN = 1024
HALF = DK // 2
BF = jnp.bfloat16
F32 = jnp.float32
STREAMS = 2
CHUNK = 256


def rms_rows(row_block, gain_vec):
    values = row_block.astype(F32)
    scale = lax.rsqrt(jnp.mean(values * values, axis=-1, keepdims=True) + 1e-06)
    return (values * scale * gain_vec).astype(BF)


def even_odd(matrix):
    rows = matrix.shape[0]
    new = jnp.arange(DK, dtype=jnp.int32)
    old = jnp.where(new < HALF, 2 * new, 2 * (new - HALF) + 1)
    one_hot = (jnp.arange(DK, dtype=jnp.int32)[:, None] == old[None, :]).astype(BF)
    heads = matrix.reshape(rows * H, DK)
    return jnp.dot(heads, one_hot, preferred_element_type=F32).astype(BF).reshape(rows, H * DK)


def by_owner(matrix, width, share, mp_count):
    rows = matrix.shape[0]
    if share > 1:
        heads = jnp.repeat(matrix.reshape(rows, H, width), share, axis=1)
        return heads.transpose(1, 0, 2)
    return matrix.reshape(rows, mp_count, -1).transpose(1, 0, 2)


def assemble_kernel(scalars, *refs):
    pieces, out_ref = refs[:-1], refs[-1]
    rows = pieces[0].shape[0]
    for step, piece in enumerate(pieces):
        place = lax.rem(scalars[0] - step + len(pieces), len(pieces))
        out_ref[pl.ds(pl.multiple_of(place * rows, rows), rows), :] = piece[...]


def in_order(pieces, index):
    rows, width = pieces[0].shape
    grid_spec = pltpu.PrefetchScalarGridSpec(
        num_scalar_prefetch=1,
        grid=(1,),
        in_specs=[pl.BlockSpec((rows, width), lambda i, s: (0, 0))] * len(pieces),
        out_specs=pl.BlockSpec((rows * len(pieces), width), lambda i, s: (0, 0)),
    )
    return pl.pallas_call(
        assemble_kernel,
        grid_spec=grid_spec,
        out_shape=jax.ShapeDtypeStruct((rows * len(pieces), width), BF),
        compiler_params=pltpu.CompilerParams(vmem_limit_bytes=16 * 2**20),
        name="assemble",
    )(index.reshape(1).astype(jnp.int32), *pieces)


def exchanged(block, index, count):
    pieces = []
    for shift in range(count):
        piece = lax.dynamic_index_in_dim(block, (index + shift) % count, 0, keepdims=False)
        if shift:
            piece = lax.ppermute(piece, "mp", [(i, (i + shift) % count) for i in range(count)])
        pieces.append(piece)
    return pieces


def stacked(refs):
    return jnp.concatenate([ref[...] for ref in refs], axis=0)


def chunk(i, size=CHUNK):
    return pl.ds(pl.multiple_of(i * size, size), size)


def project_kernel(heads, scalars, *refs):
    halves, (gain_ref, cos_ref, sin_ref, w_ref, normed_ref, out_ref) = refs[:-6], refs[-6:]
    wq = heads * DK
    normed_ref[...] = rms_rows(stacked(halves), gain_ref[...])

    def turn(h, _):
        both = jnp.dot(normed_ref[...], w_ref[:, chunk(h)], preferred_element_type=F32)
        a, b = both[:, :HALF], both[:, HALF:]
        cos, sin = cos_ref[...], sin_ref[...]
        scale = jnp.where(h < heads, DK**-0.5, 1.0)
        out_ref[:, pl.ds(pl.multiple_of(h * DK, DK), HALF)] = ((a * cos - b * sin) * scale).astype(BF)
        out_ref[:, pl.ds(pl.multiple_of(h * DK + HALF, HALF), HALF)] = ((b * cos + a * sin) * scale).astype(BF)
        return _

    def plain(i, _):
        band = chunk(i, DV)
        out_ref[:, band] = jnp.dot(normed_ref[...], w_ref[:, band], preferred_element_type=F32).astype(BF)
        return _

    lax.fori_loop(0, 2 * heads, turn, 0)
    lax.fori_loop(2 * wq // DV, out_ref.shape[1] // DV, plain, 0)


def project(halves, place, gain, cos, sin, w, heads):
    half, width = halves[0].shape
    rows = half * len(halves)
    out_width = w.shape[1]
    grid_spec = pltpu.PrefetchScalarGridSpec(
        num_scalar_prefetch=1,
        grid=(1,),
        in_specs=[pl.BlockSpec((half, width), lambda i, s: (0, 0))] * len(halves)
        + [
            pl.BlockSpec((1, width), lambda i, s: (0, 0)),
            pl.BlockSpec((rows, HALF), lambda i, s: (s[0], 0)),
            pl.BlockSpec((rows, HALF), lambda i, s: (s[0], 0)),
            pl.BlockSpec(w.shape, lambda i, s: (0, 0), pipeline_mode=pl.Buffered(1)),
        ],
        out_specs=[
            pl.BlockSpec((rows, width), lambda i, s: (0, 0)),
            pl.BlockSpec((rows, out_width), lambda i, s: (0, 0)),
        ],
    )
    return pl.pallas_call(
        lambda *refs: project_kernel(heads, *refs),
        grid_spec=grid_spec,
        out_shape=[pltpu.HBM((rows, width), BF), pltpu.HBM((rows, out_width), BF)],
        compiler_params=pltpu.CompilerParams(vmem_limit_bytes=20 * 2**20),
        cost_estimate=pl.CostEstimate(flops=rows * width * out_width // 2, bytes_accessed=2**20, transcendentals=0),
        name="project",
    )(place.reshape(1).astype(jnp.int32), *halves, gain.reshape(1, -1), cos, sin, w)


def retention_kernel(dims, scalars, run_col, run_row, x_hbm, *refs):
    heads, share, wq, wv, wg, count, own = dims
    blocks, w_hbm, out_refs = refs[:count], refs[count], refs[count + 1 : -7]
    held_ref, x_ref, kept_ref, gated_ref, wg_ref, wo_ref, arrived = refs[-7:]
    rows, width = x_ref.shape
    order = [own] + [k for k in range(count) if k != own]
    copies = [pltpu.make_async_copy(blocks[k], held_ref.at[k], arrived.at[k]) for k in order]
    copies += [
        pltpu.make_async_copy(x_hbm, x_ref, arrived.at[count]),
        pltpu.make_async_copy(w_hbm.at[:, :wg], wg_ref, arrived.at[count + 1]),
        pltpu.make_async_copy(w_hbm.at[:, wg:], wo_ref, arrived.at[count + 2]),
    ]
    for copy in copies:
        copy.start()
    device = scalars[2]
    block = lax.rem(device - own + count, count)
    live = block * rows + lax.broadcasted_iota(jnp.int32, (rows, 1), 0) < scalars[0]

    def add(past, held, first):
        for h in range(heads):
            scores = lax.dot_general(
                held_ref[own, :, h * DK : (h + 1) * DK],
                held_ref[past, :, wq + h * DK : wq + (h + 1) * DK],
                (((1,), (1,)), ((), ())),
                preferred_element_type=F32,
            )
            gap = run_col[:, h : h + 1] - run_row[held, h : h + 1, :]
            if first:
                t = lax.broadcasted_iota(jnp.int32, (rows, rows), 0)
                s = lax.broadcasted_iota(jnp.int32, (rows, rows), 1)
                gap = jnp.where(t >= s, gap, -jnp.inf)
            weights = (scores * jnp.exp(gap)).astype(BF)
            values = held_ref[past, :, 2 * wq + h * DV : 2 * wq + (h + 1) * DV]
            more = jnp.dot(weights, values, preferred_element_type=F32)
            place = slice(h * DV, (h + 1) * DV)
            kept_ref[:, place] = more if first else kept_ref[:, place] + more

    copies[0].wait()
    add(own, block, True)
    for copy in copies[1:count]:
        copy.wait()

    def earlier(held, _):
        add(lax.rem(device - held + count, count), held, False)
        return _

    lax.fori_loop(0, block, earlier, 0)

    for h in range(heads):
        kept = kept_ref[:, h * DV : (h + 1) * DV]
        mean = jnp.mean(kept, axis=-1, keepdims=True)
        spread = jnp.mean(kept * kept, axis=-1, keepdims=True) - mean * mean
        normed = (kept - mean) * lax.rsqrt(spread + 1e-05)
        if share > 1:
            mine = normed[:, :wg]
            for bit in range(1, share):
                mine = jnp.where(scalars[1] == bit, normed[:, bit * wg : (bit + 1) * wg], mine)
            kept_ref[:, :wg] = mine
        else:
            kept_ref[:, h * DV : (h + 1) * DV] = normed

    copies[count].wait()
    copies[count + 1].wait()

    wide = min(wg, 2 * CHUNK)

    def gating(i, _):
        band = chunk(i, wide)
        gate = jnp.dot(x_ref[...], wg_ref[:, band], preferred_element_type=F32).astype(BF).astype(F32)
        gate = gate / (1.0 + jnp.exp(-gate))
        gated_ref[:, band] = jnp.where(live, gate * kept_ref[:, band], 0.0).astype(BF)
        return _

    lax.fori_loop(0, wg // wide, gating, 0)
    copies[count + 2].wait()
    half = rows // len(out_refs)

    def leaving(i, _):
        band = chunk(i, 2 * CHUNK)
        branch = lax.dot_general(
            gated_ref[...], wo_ref[band, :], (((1,), (1,)), ((), ())), preferred_element_type=F32
        ).astype(BF)
        for k, out_ref in enumerate(out_refs):
            out_ref[:, band] = branch[k * half : (k + 1) * half]
        return _

    lax.fori_loop(0, width // (2 * CHUNK), leaving, 0)


def retention(own, index, x, running, length, partner, blocks, w, heads, share):
    count, (rows, width) = len(blocks), x.shape
    wq, wv, wg = heads * DK, heads * DV, w.shape[1] // 2
    dims = (heads, share, wq, wv, wg, count, own)
    scalars = jnp.stack([length, partner, index]).astype(jnp.int32)
    x, w, *blocks = [pltpu.with_memory_space_constraint(a, pltpu.HBM) for a in (x, w, *blocks)]
    by_row = running.T.reshape(heads, count, rows).transpose(1, 0, 2)
    grid_spec = pltpu.PrefetchScalarGridSpec(
        num_scalar_prefetch=1,
        grid=(1,),
        in_specs=[
            pl.BlockSpec((rows, heads), lambda i, s: (lax.rem(s[2] - own + count, count), 0)),
            pl.BlockSpec(by_row.shape, lambda i, s: (0, 0, 0)),
        ]
        + [pl.BlockSpec(memory_space=pl.ANY)] * (count + 2),
        out_specs=[pl.BlockSpec((rows // STREAMS, width), lambda i, s: (0, 0))] * STREAMS,
        scratch_shapes=[
            pltpu.VMEM((count, *blocks[0].shape), BF),
            pltpu.VMEM((rows, width), BF),
            pltpu.VMEM((rows, wv), F32),
            pltpu.VMEM((rows, wg), BF),
            pltpu.VMEM((width, wg), BF),
            pltpu.VMEM((width, wg), BF),
            pltpu.SemaphoreType.DMA((count + 3,)),
        ],
    )
    return pl.pallas_call(
        lambda *refs: retention_kernel(dims, *refs),
        grid_spec=grid_spec,
        out_shape=[jax.ShapeDtypeStruct((rows // STREAMS, width), BF)] * STREAMS,
        compiler_params=pltpu.CompilerParams(vmem_limit_bytes=24 * 2**20),
        cost_estimate=pl.CostEstimate(flops=3 * 10**9, bytes_accessed=2**20, transcendentals=10**5),
        name="retention",
    )(scalars, running, by_row, x, *blocks, w)


def middle_kernel(came_ref, part_ref, token_ref, gain_ref, residual_ref, normed_ref):
    branch = came_ref[...].astype(F32) + part_ref[...].astype(F32)
    residual_ref[...] = (token_ref[...].astype(F32) + branch).astype(BF)
    normed_ref[...] = rms_rows(residual_ref[...], gain_ref[...])


def middle(came, part, tokens, gain):
    rows, width = tokens.shape
    step = min(rows, 64)
    block = pl.BlockSpec((step, width), lambda i: (i, 0))
    return pl.pallas_call(
        middle_kernel,
        grid=(rows // step,),
        in_specs=[block, block, block, pl.BlockSpec((1, width), lambda i: (0, 0))],
        out_specs=[block, block],
        out_shape=[jax.ShapeDtypeStruct((rows, width), BF)] * 2,
        compiler_params=pltpu.CompilerParams(vmem_limit_bytes=16 * 2**20),
        name="middle",
    )(came, part, tokens, gain.reshape(1, -1))


def ffn_kernel(count, scalars, *refs):
    w_ref, out_ref, x_ref = refs[count], refs[-2], refs[-1]
    x_ref[...] = stacked(refs[:count])
    wide = min(out_ref.shape[1], 2 * CHUNK)
    chunks = out_ref.shape[1] // wide

    def one(i, _):
        gate = jnp.dot(x_ref[...], w_ref[:, chunk(i, wide)], preferred_element_type=F32)
        up = jnp.dot(x_ref[...], w_ref[:, chunk(i + chunks, wide)], preferred_element_type=F32)
        out_ref[:, chunk(i, wide)] = (gate / (1.0 + jnp.exp(-gate)) * up).astype(BF)
        return _

    lax.fori_loop(0, chunks, one, 0)


def ffn(halves, place, w, held):
    half, width = halves[0].shape
    rows = half * len(halves)
    out_width = w.shape[1] // 2
    extra = [] if held is None else [held]
    grid_spec = pltpu.PrefetchScalarGridSpec(
        num_scalar_prefetch=1,
        grid=(1,),
        in_specs=[pl.BlockSpec((half, width), lambda i, s: (0, 0))] * len(halves)
        + [pl.BlockSpec(w.shape, lambda i, s: (0, 0))]
        + [pl.BlockSpec(memory_space=pl.ANY)] * len(extra),
        out_specs=pl.BlockSpec((rows, out_width), lambda i, s: (s[0], 0)),
        scratch_shapes=[pltpu.VMEM((rows, width), BF)],
    )
    return pl.pallas_call(
        lambda *refs: ffn_kernel(len(halves), *refs),
        grid_spec=grid_spec,
        out_shape=jax.ShapeDtypeStruct((SPAN, out_width), BF),
        input_output_aliases={len(halves) + 2: 0} if extra else {},
        compiler_params=pltpu.CompilerParams(vmem_limit_bytes=18 * 2**20),
        cost_estimate=pl.CostEstimate(
            flops=2 * rows * width * w.shape[1], bytes_accessed=2 * w.size, transcendentals=rows * out_width
        ),
        name="ffn",
    )(place.reshape(1).astype(jnp.int32), *halves, w, *extra)


def per_device(
    tokens, norm_gain, mlp_gain, lengths, log_decay,
    query_master, key_master, value_master, swish_master, output_master, ffn_gate_master, ffn_up_master,
):
    mp_count = lax.axis_size("mp")
    mp_index = lax.axis_index("mp")
    share = max(1, mp_count // H)
    heads = max(1, H // mp_count)

    angles = jnp.arange(SPAN, dtype=jnp.int32).astype(F32)[:, None] * jnp.exp(
        (2 * jnp.arange(HALF, dtype=jnp.int32)).astype(F32) * (-math.log(10000.0) / DK)
    )
    cos, sin = jnp.cos(angles), jnp.sin(angles)
    first_head = mp_index // share * heads
    running = jnp.cumsum(lax.dynamic_slice_in_dim(log_decay, first_head, heads, 1), axis=0)

    qkv_pieces = exchanged(
        jnp.concatenate(
            [
                by_owner(even_odd(query_master.astype(BF)), DK, share, mp_count),
                by_owner(even_odd(key_master.astype(BF)), DK, share, mp_count),
                by_owner(value_master.astype(BF), DV, share, mp_count),
            ],
            axis=2,
        ),
        mp_index,
        mp_count,
    )
    gate_out_block = jnp.concatenate(
        [by_owner(swish_master.astype(BF), DV, 1, mp_count), by_owner(output_master.astype(BF).T, DV, 1, mp_count)],
        axis=2,
    )
    gate_out_block, qkv_pieces = lax.optimization_barrier((gate_out_block, qkv_pieces))
    gate_out_pieces = exchanged(gate_out_block, mp_index, mp_count)
    qkv_rows = in_order(qkv_pieces, mp_index)
    w_qkv = lax.all_gather(qkv_rows, "dp", axis=0, tiled=True)

    order = [(i, (i + 1) % mp_count) for i in range(mp_count)]

    def onward(halves):
        return [lax.ppermute(half, "mp", order) for half in halves]

    def projected(step):
        return project(blocks[step], (mp_index - step) % mp_count, norm_gain, cos, sin, w_qkv, heads)

    def held_back(later, *first):
        return lax.optimization_barrier((later, first))[0]

    half = tokens.shape[0] // STREAMS
    token_halves = [tokens[k * half : (k + 1) * half] for k in range(STREAMS)]
    masters = held_back((ffn_gate_master, ffn_up_master), qkv_rows)
    ffn_block = jnp.concatenate([by_owner(m.astype(BF), DV, 1, mp_count) for m in masters], axis=2)
    blocks, done = [held_back(token_halves, qkv_rows)], []
    for step in range(1, mp_count):
        blocks.append(onward(blocks[-1]))
        if step == 1:
            blocks[1] = [held_back(h, ffn_block) for h in blocks[1]]
        else:
            done.append(projected(step - 2))
            if step < mp_count - 1:
                blocks[step] = [held_back(h, done[-1]) for h in blocks[step]]
            if step == 2:
                w_gate_out = lax.all_gather(in_order(gate_out_pieces, mp_index), "dp", axis=0, tiled=True)
    done.append(projected(mp_count - 2))
    ffn_block, blocks[-1] = held_back((ffn_block, blocks[-1]), done, blocks[-1])
    ffn_pieces = exchanged(ffn_block, mp_index, mp_count)
    done.append(projected(mp_count - 1))
    normed, qkv = [d[0] for d in done], [d[1] for d in done]

    for step in range(mp_count):
        own = (1 + step) % mp_count
        parts = retention(
            own, mp_index, normed[own], running, lengths[0], mp_index % share, qkv, w_gate_out, heads, share
        )
        if step < mp_count - 1:
            later = (2 + step) % mp_count
            normed[later] = held_back(normed[later], parts)
        if step == 0:
            ffn_pieces = held_back(ffn_pieces, parts)
            w_ffn = lax.all_gather(in_order(ffn_pieces, mp_index), "dp", axis=0, tiled=True)
            totals = parts
        elif step < mp_count - 1:
            totals = [(c.astype(F32) + p.astype(F32)).astype(BF) for c, p in zip(came, parts)]
        if step < mp_count - 1:
            came = onward(totals)
    finished = [middle(c, p, t, mlp_gain) for c, p, t in zip(came, parts, token_halves)]
    residual = jnp.concatenate([f[0] for f in finished], axis=0)
    moving = [f[1] for f in finished]
    hidden = None
    for step in range(mp_count):
        here = moving
        if step < mp_count - 1:
            arriving = onward(moving)
        hidden = ffn(here, (mp_index - step) % mp_count, w_ffn, hidden)
        if step < mp_count - 1:
            moving = [held_back(h, hidden) for h in arriving] if step else arriving
    return residual, hidden


def solution(mesh):
    rows, columns = P(("dp", "mp"), None), P(None, ("dp", "mp"))
    placed = (rows, P(), P(), P("dp"), P("dp", None), rows, rows, rows, rows, columns, rows, rows)
    return jax.shard_map(
        per_device, mesh=mesh, in_specs=placed, out_specs=(rows, P("dp", "mp")), check_vma=False
    )
```

```python
import functools
import math

import jax
import jax.numpy as jnp
from jax import lax
from jax.experimental import pallas as pl
from jax.experimental.pallas import tpu as pltpu
from jax.sharding import PartitionSpec as P

H = 8
DK = 256
DV = 512
SPAN = 1024
HALF = DK // 2
BF = jnp.bfloat16
F32 = jnp.float32
STREAMS = 2
CHUNK = 256


def rms_rows(row_block, gain_vec):
    values = row_block.astype(F32)
    scale = lax.rsqrt(jnp.mean(values * values, axis=-1, keepdims=True) + 1e-06)
    return (values * scale * gain_vec).astype(BF)


def even_odd(matrix):
    rows = matrix.shape[0]
    new = jnp.arange(DK, dtype=jnp.int32)
    old = jnp.where(new < HALF, 2 * new, 2 * (new - HALF) + 1)
    one_hot = (jnp.arange(DK, dtype=jnp.int32)[:, None] == old[None, :]).astype(BF)
    heads = matrix.reshape(rows * H, DK)
    return jnp.dot(heads, one_hot, preferred_element_type=F32).astype(BF).reshape(rows, H * DK)


def by_owner(matrix, width, share, mp_count):
    rows = matrix.shape[0]
    if share > 1:
        heads = jnp.repeat(matrix.reshape(rows, H, width), share, axis=1)
        return heads.transpose(1, 0, 2)
    return matrix.reshape(rows, mp_count, -1).transpose(1, 0, 2)


def assemble_kernel(scalars, *refs):
    pieces, out_ref = refs[:-1], refs[-1]
    rows = pieces[0].shape[0]
    for step, piece in enumerate(pieces):
        place = lax.rem(scalars[0] - step + len(pieces), len(pieces))
        out_ref[pl.ds(pl.multiple_of(place * rows, rows), rows), :] = piece[...]


def in_order(pieces, index):
    rows, width = pieces[0].shape
    grid_spec = pltpu.PrefetchScalarGridSpec(
        num_scalar_prefetch=1,
        grid=(1,),
        in_specs=[pl.BlockSpec((rows, width), lambda i, s: (0, 0))] * len(pieces),
        out_specs=pl.BlockSpec((rows * len(pieces), width), lambda i, s: (0, 0)),
    )
    return pl.pallas_call(
        assemble_kernel,
        grid_spec=grid_spec,
        out_shape=jax.ShapeDtypeStruct((rows * len(pieces), width), BF),
        compiler_params=pltpu.CompilerParams(vmem_limit_bytes=16 * 2**20),
        name="assemble",
    )(index.reshape(1).astype(jnp.int32), *pieces)


def exchanged(block, index, count):
    pieces = []
    for shift in range(count):
        piece = lax.dynamic_index_in_dim(block, (index + shift) % count, 0, keepdims=False)
        if shift:
            piece = lax.ppermute(piece, "mp", [(i, (i + shift) % count) for i in range(count)])
        pieces.append(piece)
    return pieces


def stacked(refs):
    return jnp.concatenate([ref[...] for ref in refs], axis=0)


def chunk(i, size=CHUNK):
    return pl.ds(pl.multiple_of(i * size, size), size)


def project_kernel(heads, scalars, *refs):
    halves, (gain_ref, cos_ref, sin_ref, w_ref, normed_ref, out_ref) = refs[:-6], refs[-6:]
    wq = heads * DK
    normed_ref[...] = rms_rows(stacked(halves), gain_ref[...])

    def turn(h, _):
        both = jnp.dot(normed_ref[...], w_ref[:, chunk(h)], preferred_element_type=F32)
        a, b = both[:, :HALF], both[:, HALF:]
        cos, sin = cos_ref[...], sin_ref[...]
        scale = jnp.where(h < heads, DK**-0.5, 1.0)
        out_ref[:, pl.ds(pl.multiple_of(h * DK, DK), HALF)] = ((a * cos - b * sin) * scale).astype(BF)
        out_ref[:, pl.ds(pl.multiple_of(h * DK + HALF, HALF), HALF)] = ((b * cos + a * sin) * scale).astype(BF)
        return _

    def plain(i, _):
        band = chunk(i, DV)
        out_ref[:, band] = jnp.dot(normed_ref[...], w_ref[:, band], preferred_element_type=F32).astype(BF)
        return _

    lax.fori_loop(0, 2 * heads, turn, 0)
    lax.fori_loop(2 * wq // DV, out_ref.shape[1] // DV, plain, 0)


def project(halves, place, gain, cos, sin, w, heads):
    half, width = halves[0].shape
    rows = half * len(halves)
    out_width = w.shape[1]
    grid_spec = pltpu.PrefetchScalarGridSpec(
        num_scalar_prefetch=1,
        grid=(1,),
        in_specs=[pl.BlockSpec((half, width), lambda i, s: (0, 0))] * len(halves)
        + [
            pl.BlockSpec((1, width), lambda i, s: (0, 0)),
            pl.BlockSpec((rows, HALF), lambda i, s: (s[0], 0)),
            pl.BlockSpec((rows, HALF), lambda i, s: (s[0], 0)),
            pl.BlockSpec(w.shape, lambda i, s: (0, 0), pipeline_mode=pl.Buffered(1)),
        ],
        out_specs=[
            pl.BlockSpec((rows, width), lambda i, s: (0, 0)),
            pl.BlockSpec((rows, out_width), lambda i, s: (0, 0)),
        ],
    )
    return pl.pallas_call(
        lambda *refs: project_kernel(heads, *refs),
        grid_spec=grid_spec,
        out_shape=[pltpu.HBM((rows, width), BF), pltpu.HBM((rows, out_width), BF)],
        compiler_params=pltpu.CompilerParams(vmem_limit_bytes=20 * 2**20),
        cost_estimate=pl.CostEstimate(flops=rows * width * out_width // 2, bytes_accessed=2**20, transcendentals=0),
        name="project",
    )(place.reshape(1).astype(jnp.int32), *halves, gain.reshape(1, -1), cos, sin, w)


def retention_kernel(dims, scalars, run_col, run_row, x_hbm, *refs):
    heads, share, wq, wv, wg, count, own = dims
    blocks, w_hbm, out_refs = refs[:count], refs[count], refs[count + 1 : -7]
    held_ref, x_ref, kept_ref, gated_ref, wg_ref, wo_ref, arrived = refs[-7:]
    rows, width = x_ref.shape
    order = [own] + [k for k in range(count) if k != own]
    copies = [pltpu.make_async_copy(blocks[k], held_ref.at[k], arrived.at[k]) for k in order]
    copies += [
        pltpu.make_async_copy(x_hbm, x_ref, arrived.at[count]),
        pltpu.make_async_copy(w_hbm.at[:, :wg], wg_ref, arrived.at[count + 1]),
        pltpu.make_async_copy(w_hbm.at[:, wg:], wo_ref, arrived.at[count + 2]),
    ]
    for copy in copies:
        copy.start()
    device = scalars[2]
    block = lax.rem(device - own + count, count)
    live = block * rows + lax.broadcasted_iota(jnp.int32, (rows, 1), 0) < scalars[0]

    def add(past, held, first):
        for h in range(heads):
            scores = lax.dot_general(
                held_ref[own, :, h * DK : (h + 1) * DK],
                held_ref[past, :, wq + h * DK : wq + (h + 1) * DK],
                (((1,), (1,)), ((), ())),
                preferred_element_type=F32,
            )
            gap = run_col[:, h : h + 1] - run_row[held, h : h + 1, :]
            if first:
                t = lax.broadcasted_iota(jnp.int32, (rows, rows), 0)
                s = lax.broadcasted_iota(jnp.int32, (rows, rows), 1)
                gap = jnp.where(t >= s, gap, -jnp.inf)
            weights = (scores * jnp.exp(gap)).astype(BF)
            values = held_ref[past, :, 2 * wq + h * DV : 2 * wq + (h + 1) * DV]
            more = jnp.dot(weights, values, preferred_element_type=F32)
            place = slice(h * DV, (h + 1) * DV)
            kept_ref[:, place] = more if first else kept_ref[:, place] + more

    copies[0].wait()
    add(own, block, True)
    for copy in copies[1:count]:
        copy.wait()

    def earlier(held, _):
        add(lax.rem(device - held + count, count), held, False)
        return _

    lax.fori_loop(0, block, earlier, 0)

    for h in range(heads):
        kept = kept_ref[:, h * DV : (h + 1) * DV]
        mean = jnp.mean(kept, axis=-1, keepdims=True)
        spread = jnp.mean(kept * kept, axis=-1, keepdims=True) - mean * mean
        normed = (kept - mean) * lax.rsqrt(spread + 1e-05)
        if share > 1:
            mine = normed[:, :wg]
            for bit in range(1, share):
                mine = jnp.where(scalars[1] == bit, normed[:, bit * wg : (bit + 1) * wg], mine)
            kept_ref[:, :wg] = mine
        else:
            kept_ref[:, h * DV : (h + 1) * DV] = normed

    copies[count].wait()
    copies[count + 1].wait()

    wide = min(wg, 4 * CHUNK)

    def gating(i, _):
        band = chunk(i, wide)
        gate = jnp.dot(x_ref[...], wg_ref[:, band], preferred_element_type=F32).astype(BF).astype(F32)
        gate = gate / (1.0 + jnp.exp(-gate))
        gated_ref[:, band] = jnp.where(live, gate * kept_ref[:, band], 0.0).astype(BF)
        return _

    lax.fori_loop(0, wg // wide, gating, 0)
    copies[count + 2].wait()
    half = rows // len(out_refs)

    def leaving(i, _):
        band = chunk(i, 4 * CHUNK)
        branch = lax.dot_general(
            gated_ref[...], wo_ref[band, :], (((1,), (1,)), ((), ())), preferred_element_type=F32
        ).astype(BF)
        for k, out_ref in enumerate(out_refs):
            out_ref[:, band] = branch[k * half : (k + 1) * half]
        return _

    lax.fori_loop(0, width // (4 * CHUNK), leaving, 0)


def retention(own, index, x, running, length, partner, blocks, w, heads, share):
    count, (rows, width) = len(blocks), x.shape
    wq, wv, wg = heads * DK, heads * DV, w.shape[1] // 2
    dims = (heads, share, wq, wv, wg, count, own)
    scalars = jnp.stack([length, partner, index]).astype(jnp.int32)
    x, w, *blocks = [pltpu.with_memory_space_constraint(a, pltpu.HBM) for a in (x, w, *blocks)]
    by_row = running.T.reshape(heads, count, rows).transpose(1, 0, 2)
    grid_spec = pltpu.PrefetchScalarGridSpec(
        num_scalar_prefetch=1,
        grid=(1,),
        in_specs=[
            pl.BlockSpec((rows, heads), lambda i, s: (lax.rem(s[2] - own + count, count), 0)),
            pl.BlockSpec(by_row.shape, lambda i, s: (0, 0, 0)),
        ]
        + [pl.BlockSpec(memory_space=pl.ANY)] * (count + 2),
        out_specs=[pl.BlockSpec((rows // STREAMS, width), lambda i, s: (0, 0))] * STREAMS,
        scratch_shapes=[
            pltpu.VMEM((count, *blocks[0].shape), BF),
            pltpu.VMEM((rows, width), BF),
            pltpu.VMEM((rows, wv), F32),
            pltpu.VMEM((rows, wg), BF),
            pltpu.VMEM((width, wg), BF),
            pltpu.VMEM((width, wg), BF),
            pltpu.SemaphoreType.DMA((count + 3,)),
        ],
    )
    return pl.pallas_call(
        lambda *refs: retention_kernel(dims, *refs),
        grid_spec=grid_spec,
        out_shape=[jax.ShapeDtypeStruct((rows // STREAMS, width), BF)] * STREAMS,
        compiler_params=pltpu.CompilerParams(vmem_limit_bytes=24 * 2**20),
        cost_estimate=pl.CostEstimate(flops=3 * 10**9, bytes_accessed=2**20, transcendentals=10**5),
        name="retention",
    )(scalars, running, by_row, x, *blocks, w)


def middle_kernel(came_ref, part_ref, token_ref, gain_ref, residual_ref, normed_ref):
    branch = came_ref[...].astype(F32) + part_ref[...].astype(F32)
    residual_ref[...] = (token_ref[...].astype(F32) + branch).astype(BF)
    normed_ref[...] = rms_rows(residual_ref[...], gain_ref[...])


def middle(came, part, tokens, gain):
    rows, width = tokens.shape
    step = min(rows, 64)
    block = pl.BlockSpec((step, width), lambda i: (i, 0))
    return pl.pallas_call(
        middle_kernel,
        grid=(rows // step,),
        in_specs=[block, block, block, pl.BlockSpec((1, width), lambda i: (0, 0))],
        out_specs=[block, block],
        out_shape=[jax.ShapeDtypeStruct((rows, width), BF)] * 2,
        compiler_params=pltpu.CompilerParams(vmem_limit_bytes=16 * 2**20),
        name="middle",
    )(came, part, tokens, gain.reshape(1, -1))


def ffn_kernel(count, scalars, *refs):
    w_ref, out_ref, x_ref = refs[count], refs[-2], refs[-1]
    x_ref[...] = stacked(refs[:count])
    wide = min(out_ref.shape[1], 4 * CHUNK)
    chunks = out_ref.shape[1] // wide

    def one(i, _):
        gate = jnp.dot(x_ref[...], w_ref[:, chunk(i, wide)], preferred_element_type=F32)
        up = jnp.dot(x_ref[...], w_ref[:, chunk(i + chunks, wide)], preferred_element_type=F32)
        out_ref[:, chunk(i, wide)] = (gate / (1.0 + jnp.exp(-gate)) * up).astype(BF)
        return _

    lax.fori_loop(0, chunks, one, 0)


def ffn(halves, place, w, held):
    half, width = halves[0].shape
    rows = half * len(halves)
    out_width = w.shape[1] // 2
    extra = [] if held is None else [held]
    grid_spec = pltpu.PrefetchScalarGridSpec(
        num_scalar_prefetch=1,
        grid=(1,),
        in_specs=[pl.BlockSpec((half, width), lambda i, s: (0, 0))] * len(halves)
        + [pl.BlockSpec(w.shape, lambda i, s: (0, 0))]
        + [pl.BlockSpec(memory_space=pl.ANY)] * len(extra),
        out_specs=pl.BlockSpec((rows, out_width), lambda i, s: (s[0], 0)),
        scratch_shapes=[pltpu.VMEM((rows, width), BF)],
    )
    return pl.pallas_call(
        lambda *refs: ffn_kernel(len(halves), *refs),
        grid_spec=grid_spec,
        out_shape=jax.ShapeDtypeStruct((SPAN, out_width), BF),
        input_output_aliases={len(halves) + 2: 0} if extra else {},
        compiler_params=pltpu.CompilerParams(vmem_limit_bytes=18 * 2**20),
        cost_estimate=pl.CostEstimate(
            flops=2 * rows * width * w.shape[1], bytes_accessed=2 * w.size, transcendentals=rows * out_width
        ),
        name="ffn",
    )(place.reshape(1).astype(jnp.int32), *halves, w, *extra)


def per_device(
    tokens, norm_gain, mlp_gain, lengths, log_decay,
    query_master, key_master, value_master, swish_master, output_master, ffn_gate_master, ffn_up_master,
):
    mp_count = lax.axis_size("mp")
    mp_index = lax.axis_index("mp")
    share = max(1, mp_count // H)
    heads = max(1, H // mp_count)

    angles = jnp.arange(SPAN, dtype=jnp.int32).astype(F32)[:, None] * jnp.exp(
        (2 * jnp.arange(HALF, dtype=jnp.int32)).astype(F32) * (-math.log(10000.0) / DK)
    )
    cos, sin = jnp.cos(angles), jnp.sin(angles)
    first_head = mp_index // share * heads
    running = jnp.cumsum(lax.dynamic_slice_in_dim(log_decay, first_head, heads, 1), axis=0)

    qkv_pieces = exchanged(
        jnp.concatenate(
            [
                by_owner(even_odd(query_master.astype(BF)), DK, share, mp_count),
                by_owner(even_odd(key_master.astype(BF)), DK, share, mp_count),
                by_owner(value_master.astype(BF), DV, share, mp_count),
            ],
            axis=2,
        ),
        mp_index,
        mp_count,
    )
    gate_out_block = jnp.concatenate(
        [by_owner(swish_master.astype(BF), DV, 1, mp_count), by_owner(output_master.astype(BF).T, DV, 1, mp_count)],
        axis=2,
    )
    gate_out_block, qkv_pieces = lax.optimization_barrier((gate_out_block, qkv_pieces))
    gate_out_pieces = exchanged(gate_out_block, mp_index, mp_count)
    qkv_rows = in_order(qkv_pieces, mp_index)
    w_qkv = lax.all_gather(qkv_rows, "dp", axis=0, tiled=True)

    order = [(i, (i + 1) % mp_count) for i in range(mp_count)]

    def onward(halves):
        return [lax.ppermute(half, "mp", order) for half in halves]

    def projected(step):
        return project(blocks[step], (mp_index - step) % mp_count, norm_gain, cos, sin, w_qkv, heads)

    def held_back(later, *first):
        return lax.optimization_barrier((later, first))[0]

    half = tokens.shape[0] // STREAMS
    token_halves = [tokens[k * half : (k + 1) * half] for k in range(STREAMS)]
    masters = held_back((ffn_gate_master, ffn_up_master), qkv_rows)
    ffn_block = jnp.concatenate([by_owner(m.astype(BF), DV, 1, mp_count) for m in masters], axis=2)
    blocks, done = [held_back(token_halves, qkv_rows)], []
    for step in range(1, mp_count):
        blocks.append(onward(blocks[-1]))
        if step == 1:
            blocks[1] = [held_back(h, ffn_block) for h in blocks[1]]
        else:
            done.append(projected(step - 2))
            if step < mp_count - 1:
                blocks[step] = [held_back(h, done[-1]) for h in blocks[step]]
            if step == 2:
                w_gate_out = lax.all_gather(in_order(gate_out_pieces, mp_index), "dp", axis=0, tiled=True)
    done.append(projected(mp_count - 2))
    ffn_block, blocks[-1] = held_back((ffn_block, blocks[-1]), done, blocks[-1])
    ffn_pieces = exchanged(ffn_block, mp_index, mp_count)
    done.append(projected(mp_count - 1))
    normed, qkv = [d[0] for d in done], [d[1] for d in done]

    for step in range(mp_count):
        own = (1 + step) % mp_count
        parts = retention(
            own, mp_index, normed[own], running, lengths[0], mp_index % share, qkv, w_gate_out, heads, share
        )
        if step < mp_count - 1:
            later = (2 + step) % mp_count
            normed[later] = held_back(normed[later], parts)
        if step == 0:
            ffn_pieces = held_back(ffn_pieces, parts)
            w_ffn = lax.all_gather(in_order(ffn_pieces, mp_index), "dp", axis=0, tiled=True)
            totals = parts
        elif step < mp_count - 1:
            totals = [(c.astype(F32) + p.astype(F32)).astype(BF) for c, p in zip(came, parts)]
        if step < mp_count - 1:
            came = onward(totals)
    finished = [middle(c, p, t, mlp_gain) for c, p, t in zip(came, parts, token_halves)]
    residual = jnp.concatenate([f[0] for f in finished], axis=0)
    moving = [f[1] for f in finished]
    hidden = None
    for step in range(mp_count):
        here = moving
        if step < mp_count - 1:
            arriving = onward(moving)
        hidden = ffn(here, (mp_index - step) % mp_count, w_ffn, hidden)
        if step < mp_count - 1:
            moving = [held_back(h, hidden) for h in arriving] if step else arriving
    return residual, hidden


def solution(mesh):
    rows, columns = P(("dp", "mp"), None), P(None, ("dp", "mp"))
    placed = (rows, P(), P(), P("dp"), P("dp", None), rows, rows, rows, rows, columns, rows, rows)
    return jax.shard_map(
        per_device, mesh=mesh, in_specs=placed, out_specs=(rows, P("dp", "mp")), check_vma=False
    )
```

```python
import functools
import math

import jax
import jax.numpy as jnp
from jax import lax
from jax.experimental import pallas as pl
from jax.experimental.pallas import tpu as pltpu
from jax.sharding import PartitionSpec as P

H = 8
DK = 256
DV = 512
SPAN = 1024
HALF = DK // 2
BF = jnp.bfloat16
F32 = jnp.float32
STREAMS = 2
CHUNK = 256


def rms_rows(row_block, gain_vec):
    values = row_block.astype(F32)
    scale = lax.rsqrt(jnp.mean(values * values, axis=-1, keepdims=True) + 1e-06)
    return (values * scale * gain_vec).astype(BF)


def even_odd(matrix):
    rows = matrix.shape[0]
    new = jnp.arange(DK, dtype=jnp.int32)
    old = jnp.where(new < HALF, 2 * new, 2 * (new - HALF) + 1)
    one_hot = (jnp.arange(DK, dtype=jnp.int32)[:, None] == old[None, :]).astype(BF)
    heads = matrix.reshape(rows * H, DK)
    return jnp.dot(heads, one_hot, preferred_element_type=F32).astype(BF).reshape(rows, H * DK)


def by_owner(matrix, width, share, mp_count):
    rows = matrix.shape[0]
    if share > 1:
        heads = jnp.repeat(matrix.reshape(rows, H, width), share, axis=1)
        return heads.transpose(1, 0, 2)
    return matrix.reshape(rows, mp_count, -1).transpose(1, 0, 2)


def assemble_kernel(scalars, *refs):
    pieces, out_ref = refs[:-1], refs[-1]
    rows = pieces[0].shape[0]
    for step, piece in enumerate(pieces):
        place = lax.rem(scalars[0] - step + len(pieces), len(pieces))
        out_ref[pl.ds(pl.multiple_of(place * rows, rows), rows), :] = piece[...]


def in_order(pieces, index):
    rows, width = pieces[0].shape
    grid_spec = pltpu.PrefetchScalarGridSpec(
        num_scalar_prefetch=1,
        grid=(1,),
        in_specs=[pl.BlockSpec((rows, width), lambda i, s: (0, 0))] * len(pieces),
        out_specs=pl.BlockSpec((rows * len(pieces), width), lambda i, s: (0, 0)),
    )
    return pl.pallas_call(
        assemble_kernel,
        grid_spec=grid_spec,
        out_shape=jax.ShapeDtypeStruct((rows * len(pieces), width), BF),
        compiler_params=pltpu.CompilerParams(vmem_limit_bytes=16 * 2**20),
        name="assemble",
    )(index.reshape(1).astype(jnp.int32), *pieces)


def exchanged(block, index, count):
    pieces = []
    for shift in range(count):
        piece = lax.dynamic_index_in_dim(block, (index + shift) % count, 0, keepdims=False)
        if shift:
            piece = lax.ppermute(piece, "mp", [(i, (i + shift) % count) for i in range(count)])
        pieces.append(piece)
    return pieces


def stacked(refs):
    return jnp.concatenate([ref[...] for ref in refs], axis=0)


def chunk(i, size=CHUNK):
    return pl.ds(pl.multiple_of(i * size, size), size)


def project_kernel(heads, scalars, *refs):
    halves, (gain_ref, cos_ref, sin_ref, w_ref, normed_ref, out_ref) = refs[:-6], refs[-6:]
    wq = heads * DK
    normed_ref[...] = rms_rows(stacked(halves), gain_ref[...])

    def turn(h, _):
        both = jnp.dot(normed_ref[...], w_ref[:, chunk(h)], preferred_element_type=F32)
        a, b = both[:, :HALF], both[:, HALF:]
        cos, sin = cos_ref[...], sin_ref[...]
        scale = jnp.where(h < heads, DK**-0.5, 1.0)
        out_ref[:, pl.ds(pl.multiple_of(h * DK, DK), HALF)] = ((a * cos - b * sin) * scale).astype(BF)
        out_ref[:, pl.ds(pl.multiple_of(h * DK + HALF, HALF), HALF)] = ((b * cos + a * sin) * scale).astype(BF)
        return _

    def plain(i, _):
        band = chunk(i, DV)
        out_ref[:, band] = jnp.dot(normed_ref[...], w_ref[:, band], preferred_element_type=F32).astype(BF)
        return _

    lax.fori_loop(0, 2 * heads, turn, 0)
    lax.fori_loop(2 * wq // DV, out_ref.shape[1] // DV, plain, 0)


def project(halves, place, gain, cos, sin, w, heads):
    half, width = halves[0].shape
    rows = half * len(halves)
    out_width = w.shape[1]
    grid_spec = pltpu.PrefetchScalarGridSpec(
        num_scalar_prefetch=1,
        grid=(1,),
        in_specs=[pl.BlockSpec((half, width), lambda i, s: (0, 0))] * len(halves)
        + [
            pl.BlockSpec((1, width), lambda i, s: (0, 0)),
            pl.BlockSpec((rows, HALF), lambda i, s: (s[0], 0)),
            pl.BlockSpec((rows, HALF), lambda i, s: (s[0], 0)),
            pl.BlockSpec(w.shape, lambda i, s: (0, 0), pipeline_mode=pl.Buffered(1)),
        ],
        out_specs=[
            pl.BlockSpec((rows, width), lambda i, s: (0, 0)),
            pl.BlockSpec((rows, out_width), lambda i, s: (0, 0)),
        ],
    )
    return pl.pallas_call(
        lambda *refs: project_kernel(heads, *refs),
        grid_spec=grid_spec,
        out_shape=[pltpu.HBM((rows, width), BF), pltpu.HBM((rows, out_width), BF)],
        compiler_params=pltpu.CompilerParams(vmem_limit_bytes=20 * 2**20),
        cost_estimate=pl.CostEstimate(flops=rows * width * out_width // 2, bytes_accessed=2**20, transcendentals=0),
        name="project",
    )(place.reshape(1).astype(jnp.int32), *halves, gain.reshape(1, -1), cos, sin, w)


def retention_kernel(dims, scalars, run_col, run_row, x_hbm, *refs):
    heads, share, wq, wv, wg, count, own = dims
    blocks, w_hbm, out_refs = refs[:count], refs[count], refs[count + 1 : -7]
    held_ref, x_ref, kept_ref, gated_ref, wg_ref, wo_ref, arrived = refs[-7:]
    rows, width = x_ref.shape
    order = [own] + [k for k in range(count) if k != own]
    copies = [pltpu.make_async_copy(blocks[k], held_ref.at[k], arrived.at[k]) for k in order]
    copies += [
        pltpu.make_async_copy(x_hbm, x_ref, arrived.at[count]),
        pltpu.make_async_copy(w_hbm.at[:, :wg], wg_ref, arrived.at[count + 1]),
        pltpu.make_async_copy(w_hbm.at[:, wg:], wo_ref, arrived.at[count + 2]),
    ]
    for copy in copies:
        copy.start()
    device = scalars[2]
    block = lax.rem(device - own + count, count)
    live = block * rows + lax.broadcasted_iota(jnp.int32, (rows, 1), 0) < scalars[0]

    def add(past, held, first):
        for h in range(heads):
            scores = lax.dot_general(
                held_ref[own, :, h * DK : (h + 1) * DK],
                held_ref[past, :, wq + h * DK : wq + (h + 1) * DK],
                (((1,), (1,)), ((), ())),
                preferred_element_type=F32,
            )
            gap = run_col[:, h : h + 1] - run_row[held, h : h + 1, :]
            if first:
                t = lax.broadcasted_iota(jnp.int32, (rows, rows), 0)
                s = lax.broadcasted_iota(jnp.int32, (rows, rows), 1)
                gap = jnp.where(t >= s, gap, -jnp.inf)
            weights = (scores * jnp.exp(gap)).astype(BF)
            values = held_ref[past, :, 2 * wq + h * DV : 2 * wq + (h + 1) * DV]
            more = jnp.dot(weights, values, preferred_element_type=F32)
            place = slice(h * DV, (h + 1) * DV)
            kept_ref[:, place] = more if first else kept_ref[:, place] + more

    copies[0].wait()
    add(own, block, True)
    for copy in copies[1:count]:
        copy.wait()

    def earlier(held, _):
        add(lax.rem(device - held + count, count), held, False)
        return _

    lax.fori_loop(0, block, earlier, 0)

    for h in range(heads):
        kept = kept_ref[:, h * DV : (h + 1) * DV]
        mean = jnp.mean(kept, axis=-1, keepdims=True)
        spread = jnp.mean(kept * kept, axis=-1, keepdims=True) - mean * mean
        normed = (kept - mean) * lax.rsqrt(spread + 1e-05)
        if share > 1:
            mine = normed[:, :wg]
            for bit in range(1, share):
                mine = jnp.where(scalars[1] == bit, normed[:, bit * wg : (bit + 1) * wg], mine)
            kept_ref[:, :wg] = mine
        else:
            kept_ref[:, h * DV : (h + 1) * DV] = normed

    copies[count].wait()
    copies[count + 1].wait()

    wide = min(wg, 4 * CHUNK)

    def gating(i, _):
        band = chunk(i, wide)
        gate = jnp.dot(x_ref[...], wg_ref[:, band], preferred_element_type=F32).astype(BF).astype(F32)
        gate = gate / (1.0 + jnp.exp(-gate))
        gated_ref[:, band] = jnp.where(live, gate * kept_ref[:, band], 0.0).astype(BF)
        return _

    lax.fori_loop(0, wg // wide, gating, 0)
    copies[count + 2].wait()
    half = rows // len(out_refs)

    def leaving(i, _):
        band = chunk(i, 4 * CHUNK)
        branch = lax.dot_general(
            gated_ref[...], wo_ref[band, :], (((1,), (1,)), ((), ())), preferred_element_type=F32
        ).astype(BF)
        for k, out_ref in enumerate(out_refs):
            out_ref[:, band] = branch[k * half : (k + 1) * half]
        return _

    lax.fori_loop(0, width // (4 * CHUNK), leaving, 0)


def retention(own, index, x, running, length, partner, blocks, w, heads, share):
    count, (rows, width) = len(blocks), x.shape
    wq, wv, wg = heads * DK, heads * DV, w.shape[1] // 2
    dims = (heads, share, wq, wv, wg, count, own)
    scalars = jnp.stack([length, partner, index]).astype(jnp.int32)
    x, w, *blocks = [pltpu.with_memory_space_constraint(a, pltpu.HBM) for a in (x, w, *blocks)]
    by_row = running.T.reshape(heads, count, rows).transpose(1, 0, 2)
    grid_spec = pltpu.PrefetchScalarGridSpec(
        num_scalar_prefetch=1,
        grid=(1,),
        in_specs=[
            pl.BlockSpec((rows, heads), lambda i, s: (lax.rem(s[2] - own + count, count), 0)),
            pl.BlockSpec(by_row.shape, lambda i, s: (0, 0, 0)),
        ]
        + [pl.BlockSpec(memory_space=pl.ANY)] * (count + 2),
        out_specs=[pl.BlockSpec((rows // STREAMS, width), lambda i, s: (0, 0))] * STREAMS,
        scratch_shapes=[
            pltpu.VMEM((count, *blocks[0].shape), BF),
            pltpu.VMEM((rows, width), BF),
            pltpu.VMEM((rows, wv), F32),
            pltpu.VMEM((rows, wg), BF),
            pltpu.VMEM((width, wg), BF),
            pltpu.VMEM((width, wg), BF),
            pltpu.SemaphoreType.DMA((count + 3,)),
        ],
    )
    return pl.pallas_call(
        lambda *refs: retention_kernel(dims, *refs),
        grid_spec=grid_spec,
        out_shape=[jax.ShapeDtypeStruct((rows // STREAMS, width), BF)] * STREAMS,
        compiler_params=pltpu.CompilerParams(vmem_limit_bytes=24 * 2**20),
        cost_estimate=pl.CostEstimate(flops=3 * 10**9, bytes_accessed=2**20, transcendentals=10**5),
        name="retention",
    )(scalars, running, by_row, x, *blocks, w)


def middle_kernel(came_ref, part_ref, token_ref, gain_ref, residual_ref, normed_ref):
    branch = came_ref[...].astype(F32) + part_ref[...].astype(F32)
    residual_ref[...] = (token_ref[...].astype(F32) + branch).astype(BF)
    normed_ref[...] = rms_rows(residual_ref[...], gain_ref[...])


def middle(came, part, tokens, gain):
    rows, width = tokens.shape
    step = min(rows, 128)
    block = pl.BlockSpec((step, width), lambda i: (i, 0))
    return pl.pallas_call(
        middle_kernel,
        grid=(rows // step,),
        in_specs=[block, block, block, pl.BlockSpec((1, width), lambda i: (0, 0))],
        out_specs=[block, block],
        out_shape=[jax.ShapeDtypeStruct((rows, width), BF)] * 2,
        compiler_params=pltpu.CompilerParams(vmem_limit_bytes=16 * 2**20),
        name="middle",
    )(came, part, tokens, gain.reshape(1, -1))


def ffn_kernel(count, scalars, *refs):
    w_ref, out_ref, x_ref = refs[count], refs[-2], refs[-1]
    x_ref[...] = stacked(refs[:count])
    wide = min(out_ref.shape[1], 4 * CHUNK)
    chunks = out_ref.shape[1] // wide

    def one(i, _):
        gate = jnp.dot(x_ref[...], w_ref[:, chunk(i, wide)], preferred_element_type=F32)
        up = jnp.dot(x_ref[...], w_ref[:, chunk(i + chunks, wide)], preferred_element_type=F32)
        out_ref[:, chunk(i, wide)] = (gate / (1.0 + jnp.exp(-gate)) * up).astype(BF)
        return _

    lax.fori_loop(0, chunks, one, 0)


def ffn(halves, place, w, held):
    half, width = halves[0].shape
    rows = half * len(halves)
    out_width = w.shape[1] // 2
    extra = [] if held is None else [held]
    grid_spec = pltpu.PrefetchScalarGridSpec(
        num_scalar_prefetch=1,
        grid=(1,),
        in_specs=[pl.BlockSpec((half, width), lambda i, s: (0, 0))] * len(halves)
        + [pl.BlockSpec(w.shape, lambda i, s: (0, 0))]
        + [pl.BlockSpec(memory_space=pl.ANY)] * len(extra),
        out_specs=pl.BlockSpec((rows, out_width), lambda i, s: (s[0], 0)),
        scratch_shapes=[pltpu.VMEM((rows, width), BF)],
    )
    return pl.pallas_call(
        lambda *refs: ffn_kernel(len(halves), *refs),
        grid_spec=grid_spec,
        out_shape=jax.ShapeDtypeStruct((SPAN, out_width), BF),
        input_output_aliases={len(halves) + 2: 0} if extra else {},
        compiler_params=pltpu.CompilerParams(vmem_limit_bytes=18 * 2**20),
        cost_estimate=pl.CostEstimate(
            flops=2 * rows * width * w.shape[1], bytes_accessed=2 * w.size, transcendentals=rows * out_width
        ),
        name="ffn",
    )(place.reshape(1).astype(jnp.int32), *halves, w, *extra)


def per_device(
    tokens, norm_gain, mlp_gain, lengths, log_decay,
    query_master, key_master, value_master, swish_master, output_master, ffn_gate_master, ffn_up_master,
):
    mp_count = lax.axis_size("mp")
    mp_index = lax.axis_index("mp")
    share = max(1, mp_count // H)
    heads = max(1, H // mp_count)

    angles = jnp.arange(SPAN, dtype=jnp.int32).astype(F32)[:, None] * jnp.exp(
        (2 * jnp.arange(HALF, dtype=jnp.int32)).astype(F32) * (-math.log(10000.0) / DK)
    )
    cos, sin = jnp.cos(angles), jnp.sin(angles)
    first_head = mp_index // share * heads
    running = jnp.cumsum(lax.dynamic_slice_in_dim(log_decay, first_head, heads, 1), axis=0)

    qkv_pieces = exchanged(
        jnp.concatenate(
            [
                by_owner(even_odd(query_master.astype(BF)), DK, share, mp_count),
                by_owner(even_odd(key_master.astype(BF)), DK, share, mp_count),
                by_owner(value_master.astype(BF), DV, share, mp_count),
            ],
            axis=2,
        ),
        mp_index,
        mp_count,
    )
    gate_out_block = jnp.concatenate(
        [by_owner(swish_master.astype(BF), DV, 1, mp_count), by_owner(output_master.astype(BF).T, DV, 1, mp_count)],
        axis=2,
    )
    gate_out_block, qkv_pieces = lax.optimization_barrier((gate_out_block, qkv_pieces))
    gate_out_pieces = exchanged(gate_out_block, mp_index, mp_count)
    qkv_rows = in_order(qkv_pieces, mp_index)
    w_qkv = lax.all_gather(qkv_rows, "dp", axis=0, tiled=True)

    order = [(i, (i + 1) % mp_count) for i in range(mp_count)]

    def onward(halves):
        return [lax.ppermute(half, "mp", order) for half in halves]

    def projected(step):
        return project(blocks[step], (mp_index - step) % mp_count, norm_gain, cos, sin, w_qkv, heads)

    def held_back(later, *first):
        return lax.optimization_barrier((later, first))[0]

    half = tokens.shape[0] // STREAMS
    token_halves = [tokens[k * half : (k + 1) * half] for k in range(STREAMS)]
    masters = held_back((ffn_gate_master, ffn_up_master), qkv_rows)
    ffn_block = jnp.concatenate([by_owner(m.astype(BF), DV, 1, mp_count) for m in masters], axis=2)
    blocks, done = [held_back(token_halves, qkv_rows)], []
    for step in range(1, mp_count):
        blocks.append(onward(blocks[-1]))
        if step == 1:
            blocks[1] = [held_back(h, ffn_block) for h in blocks[1]]
        else:
            done.append(projected(step - 2))
            if step < mp_count - 1:
                blocks[step] = [held_back(h, done[-1]) for h in blocks[step]]
            if step == 2:
                w_gate_out = lax.all_gather(in_order(gate_out_pieces, mp_index), "dp", axis=0, tiled=True)
    done.append(projected(mp_count - 2))
    ffn_block, blocks[-1] = held_back((ffn_block, blocks[-1]), done, blocks[-1])
    ffn_pieces = exchanged(ffn_block, mp_index, mp_count)
    done.append(projected(mp_count - 1))
    normed, qkv = [d[0] for d in done], [d[1] for d in done]

    for step in range(mp_count):
        own = (1 + step) % mp_count
        parts = retention(
            own, mp_index, normed[own], running, lengths[0], mp_index % share, qkv, w_gate_out, heads, share
        )
        if step < mp_count - 1:
            later = (2 + step) % mp_count
            normed[later] = held_back(normed[later], parts)
        if step == 0:
            ffn_pieces = held_back(ffn_pieces, parts)
            w_ffn = lax.all_gather(in_order(ffn_pieces, mp_index), "dp", axis=0, tiled=True)
            totals = parts
        elif step < mp_count - 1:
            totals = [(c.astype(F32) + p.astype(F32)).astype(BF) for c, p in zip(came, parts)]
        if step < mp_count - 1:
            came = onward(totals)
    finished = [middle(c, p, t, mlp_gain) for c, p, t in zip(came, parts, token_halves)]
    residual = jnp.concatenate([f[0] for f in finished], axis=0)
    moving = [f[1] for f in finished]
    hidden = None
    for step in range(mp_count):
        here = moving
        if step < mp_count - 1:
            arriving = onward(moving)
        hidden = ffn(here, (mp_index - step) % mp_count, w_ffn, hidden)
        if step < mp_count - 1:
            moving = [held_back(h, hidden) for h in arriving] if step else arriving
    return residual, hidden


def solution(mesh):
    rows, columns = P(("dp", "mp"), None), P(None, ("dp", "mp"))
    placed = (rows, P(), P(), P("dp"), P("dp", None), rows, rows, rows, rows, columns, rows, rows)
    return jax.shard_map(
        per_device, mesh=mesh, in_specs=placed, out_specs=(rows, P("dp", "mp")), check_vma=False
    )
```
